512 devices in a mesh: batch: 8 (over z_lo, core), item: 64 (over x, z_hi, y).
Axes of the slice: x: 4, y: 4, z: 16 (z_hi: 4, z_lo: 4; z = z_hi * 4 + z_lo), core: 2. Of those that a mesh axis runs over, the one named last changes fastest.
Arguments:
- hidden: bfloat16 [4096, 256], P(('batch', 'item')), may hold values from -80 to 80
- item_table: bfloat16 [491520, 256], P('item'), may hold values from -0.75 to 0.75
- bucket_blocks: int32 [64, 128], P('batch'), may hold values from 0 to 959, as said below
- targets: int32 [4096], P('batch'), may hold values from 0 to 491519, as said below
- row_weight: float32 [4096], P('batch'), may hold values from 0.5 to 1.5
Outputs:
- row_loss: float32 [4096], P(('batch', 'item'))
- grad_hidden: bfloat16 [4096, 256], P(('batch', 'item'))
- grad_table: bfloat16 [256, 491520], P('batch', 'item')
The draws below stay inside these ranges and needn't reach their ends.
Inputs may be any that keep to these rules, and one draw needn't show every extreme that they name: `bucket_blocks`: each row lists 128 distinct blocks; block j lies on item index j // 15; at most 8 blocks of a row lie on one item index, and in every row some index holds exactly 8. targets[r] lies in a block listed in row r // 64 of bucket_blocks.
All inputs are finite; a program needn't handle non-finite values.
Results may differ from the reference program's by a relative error of at most 0.0055.
Values may be sent and summed in bfloat16 or wider, within the bound.
A program may use at most 128 MiB of HBM per device.

```python
import math
import jax
import jax.numpy as jnp
from jax import lax

D = 256
BLK = 512
ITEM_DEV = 7680
MOST = 8
BR = 64
ROW_DEV = 512
ITEMS = 491520
K = 128
ROWS = 4096
N_BATCH = 8
N_ITEM = 64


def block_lists(key):
    device_count = N_ITEM
    per_device = ITEM_DEV // BLK
    bucket_count = ROW_DEV * N_BATCH // BR
    positions = jnp.arange(device_count)
    counts = jnp.where(positions < device_count // 8, MOST, jnp.where(positions < 3 * device_count // 8, 2, jnp.where(positions < 7 * device_count // 8, 1, 0)))
    slot_ends = jnp.cumsum(counts)
    starts = slot_ends - counts
    slot_ids = jnp.arange(K)
    rank_of = jnp.sum(slot_ids[:, None] >= slot_ends[None, :], axis=1)
    within = slot_ids - starts[rank_of]

    def one_bucket(bucket_key):
        device_key, block_key = jax.random.split(bucket_key)
        devices = jax.random.permutation(device_key, device_count)
        inner_keys = jax.random.split(block_key, device_count)
        orders = jax.vmap(lambda inner_key: jax.random.permutation(inner_key, per_device))(inner_keys)
        return devices[rank_of] * per_device + orders[rank_of, within]
    return jax.vmap(one_bucket)(jax.random.split(key, bucket_count)).astype(jnp.int32)


def aligned_direction(key):
    direction_key = jax.random.fold_in(key, 17)
    return jnp.where(jax.random.bernoulli(direction_key, 0.5, (D,)), 1.0, -1.0).astype(jnp.float32)


def draw_bucket_blocks(key, part):
    return block_lists(key)


def draw_targets(key, part):
    listed = block_lists(key)
    key = jax.random.fold_in(key, 7)
    first_key, second_key = jax.random.split(key)
    rows_all = ROW_DEV * N_BATCH
    choose_slot = jax.random.randint(first_key, (rows_all,), 0, K)
    offset = jax.random.randint(second_key, (rows_all,), 0, BLK)
    bucket = jnp.arange(rows_all) // BR
    return (listed[bucket, choose_slot] * BLK + offset).astype(jnp.int32)


def draw_hidden(key, part):
    direction = aligned_direction(key)
    key = jax.random.fold_in(key, 11)
    value_key, scale_key, strength_key = jax.random.split(key, 3)
    array_shape = (ROW_DEV * N_BATCH, D)
    values = jnp.clip(jax.random.normal(value_key, array_shape, jnp.float32), -4.0, 4.0)
    scales = jnp.exp(jax.random.uniform(scale_key, (array_shape[0], 1), jnp.float32, math.log(0.5), math.log(3.0)))
    strength = jnp.exp(jax.random.uniform(strength_key, (array_shape[0], 1), jnp.float32, math.log(110.0), math.log(280.0)))
    aligned = direction[None, :] * (strength / (0.75 * D))
    chosen = (jnp.arange(array_shape[0]) % BR == 0)[:, None]
    return jnp.where(chosen, aligned, values * scales).astype(jnp.bfloat16)


def draw_item_table(key, part):
    direction = aligned_direction(key)
    key = jax.random.fold_in(key, 13)
    value_key, scale_key = jax.random.split(key)
    array_shape = (ITEM_DEV * N_ITEM, D)
    values = jnp.clip(jax.random.normal(value_key, array_shape, jnp.float32), -4.0, 4.0)
    scales = jnp.exp(jax.random.uniform(scale_key, (array_shape[0], 1), jnp.float32, math.log(0.5), math.log(3.0)))
    drawn = values * scales / 16.0
    offsets = (jnp.arange(array_shape[0]) % BLK)[:, None]
    drawn = jnp.where(offsets == 0, 0.75 * direction[None, :], drawn)
    drawn = jnp.where(offsets == 1, 0.7421875 * direction[None, :], drawn)
    return drawn.astype(jnp.bfloat16)


def block_scale(rng, dims, shards, least, largest):
    loudness, own = 1.0, jax.random.fold_in(rng, 6)
    for axis_at, blocks in shards:
        heights = jnp.exp(jax.random.uniform(jax.random.fold_in(own, axis_at), (blocks,), jnp.float32, least / len(shards), largest / len(shards)))
        loudness = loudness * jnp.repeat(heights, dims[axis_at] // blocks).reshape([-1 if axis == axis_at else 1 for axis in range(len(dims))])
    return loudness


def setup_inputs(seed: int = 0) -> dict:
    key_of = jax.random.split(jax.random.key(seed), 6)
    hidden = draw_hidden(jax.random.fold_in(key_of[5], 71), 0)
    item_table = draw_item_table(jax.random.fold_in(key_of[5], 71), 0)
    bucket_blocks = draw_bucket_blocks(jax.random.fold_in(key_of[5], 71), 0)
    targets = draw_targets(jax.random.fold_in(key_of[5], 71), 0)
    row_weight = jnp.clip(0.5 + 1.0 * jax.random.uniform(key_of[4], (ROWS,), jnp.float32) ** block_scale(key_of[4], (ROWS,), ((0, 8),), -0.2, 0.2), 0.5, 1.5)
    return {"hidden": hidden, "item_table": item_table, "bucket_blocks": bucket_blocks, "targets": targets, "row_weight": row_weight}


def bucket_terms(row_block, block_list, aimed_items, weights, shaped_table):
    block_panels = shaped_table[block_list].astype(jnp.float32)
    features = row_block.astype(jnp.float32)
    logit_values = jnp.einsum("qd,kid->qki", features, block_panels)
    row_max = jnp.max(logit_values, axis=(1, 2))
    row_total = jnp.sum(jnp.exp(logit_values - row_max[:, None, None]), axis=(1, 2))
    target_mask = (block_list[None, :, None] == (aimed_items // BLK)[:, None, None]) & (
        jnp.arange(BLK, dtype=jnp.int32)[None, None, :] == (aimed_items % BLK)[:, None, None])
    target_score = jnp.sum(jnp.where(target_mask, logit_values, 0.0), axis=(1, 2))
    row_loss = row_max + jnp.log(row_total) - target_score
    chance = jnp.exp(logit_values - row_max[:, None, None]) / row_total[:, None, None]
    rounded = lax.optimization_barrier((weights[:, None, None] * (chance - target_mask.astype(jnp.float32))).astype(jnp.bfloat16))
    softmax_factor = rounded.astype(jnp.float32)
    grad_rows = jnp.einsum("qki,kid->qd", softmax_factor, block_panels)
    contrib = jnp.einsum("qki,qd->kid", softmax_factor, features)
    return row_loss, grad_rows, contrib


def reference(hidden, item_table, bucket_blocks, targets, row_weight):
    shaped_table = item_table.reshape(ITEMS // BLK, BLK, D)
    bucket_group = ROW_DEV // BR
    row_groups = hidden.reshape(N_BATCH, bucket_group, BR, D)
    list_groups = bucket_blocks.reshape(N_BATCH, bucket_group, K)
    aim_groups = targets.reshape(N_BATCH, bucket_group, BR)
    weight_groups = row_weight.reshape(N_BATCH, bucket_group, BR)

    def group_step(running, pieces):
        def bucket_step(part_sum, inner_items):
            row_block, block_list, aimed_items, weights = inner_items
            row_loss, grad_rows, contrib = bucket_terms(row_block, block_list, aimed_items, weights, shaped_table)
            return part_sum.at[block_list].add(contrib), (row_loss, grad_rows)

        part_sum, outputs = lax.scan(bucket_step, jnp.zeros((ITEMS // BLK, BLK, D), jnp.float32), pieces)
        rounded = lax.optimization_barrier(part_sum.astype(jnp.bfloat16))
        return running + rounded.astype(jnp.float32), outputs

    total_grad, outputs = lax.scan(group_step, jnp.zeros((ITEMS // BLK, BLK, D), jnp.float32),
                                   (row_groups, list_groups, aim_groups, weight_groups))
    losses, grad_rows = outputs
    row_loss = losses.reshape(ROWS)
    grad_hidden = grad_rows.reshape(ROWS, D).astype(jnp.bfloat16)
    grad_table = total_grad.reshape(ITEMS, D).T.astype(jnp.bfloat16)
    return row_loss, grad_hidden, grad_table
```

```python
import functools

import jax
import jax.numpy as jnp
from jax import lax
from jax.experimental import pallas as pl
from jax.experimental.pallas import tpu as pltpu
from jax.sharding import PartitionSpec as P

MESH = pl.DeviceIdType.MESH
F32 = jnp.float32
BF16 = jnp.bfloat16

BLK = 512
NEGATIVE = -1e30
TILE = 256
LANES = 256
LAG_CORE = 2
LAG_CHIP = 5


def kernel(hid, meta, table, loss, gh_out, gt_out,
           tab, tab_t, hb, hf, ht, hp, metab, pbuf, mt, run, stx, stz, cbuf, ght, gs, gr, zs, zr,
           a_send, a_keep, a_recv, b_send, b_keep, b_recv, c_send,
           tsem, msem, zsem, xsem, sxsem, szsem, asem, bsem, csem, gxsem, gzsem):
    b = lax.axis_index("batch")
    i = lax.axis_index("item")
    zl, k = b // 2, b % 2
    par, half = zl % 2, zl // 2
    x, zh, y = i // 16, (i // 4) % 4, i % 4
    xy = x * 4 + y
    qm = half * 4 + zh
    n_half = tab.shape[0]
    n_tile = n_half // TILE
    rows = ht.shape[1]
    n_feat = tab.shape[1]
    share = rows // 2

    def z_dev(q):
        return ((par + 2 * (q // 4)) * 2 + k, x * 16 + (q % 4) * 4 + y)

    def xy_dev(v):
        return (b, (v // 4) * 16 + zh * 4 + v % 4)

    sibling = (zl * 2 + 1 - k, i)
    partner = ((zl + 1 - 2 * par) * 2 + k, i)
    other = ((par + 2 * (1 - half)) * 2 + k, i)

    def remote(src, dst, sems, j, dev):
        return pltpu.make_async_remote_copy(
            src_ref=src, dst_ref=dst, send_sem=sems.at[0, j], recv_sem=sems.at[1, j],
            device_id=dev, device_id_type=MESH)

    def loop(lo, hi, body):
        def step(j, carry):
            body(j)
            return carry
        lax.fori_loop(lo, hi, step, 0)

    table_copy = pltpu.make_async_copy(table.at[pl.ds(half * n_half, n_half), :], tab, tsem)
    table_copy.start()

    barrier = pltpu.get_barrier_semaphore()

    def greet(dev):
        pl.semaphore_signal(barrier, inc=1, device_id=dev, device_id_type=MESH)

    loop(1, 8, lambda j: greet(z_dev((qm + j) % 8)))
    loop(1, 16, lambda j: greet(xy_dev((xy + j) % 16)))
    greet(sibling)
    greet(partner)

    own = hid[...].astype(F32)
    hb[xy, qm] = jnp.concatenate([own[:, :128], own[:, 128:]], axis=0).astype(BF16)
    metab[half] = meta[...]
    pl.semaphore_wait(barrier, 24)

    loop(1, 8, lambda j: remote(hb.at[xy, qm], hb.at[xy, qm], zsem, j, z_dev((qm + j) % 8)).start())
    meta_copy = remote(metab.at[half], metab.at[half], msem, 0, other)
    meta_copy.start()

    def z_recv(j):
        q = (qm + 8 - j) % 8
        remote(hb.at[xy, q], hb.at[xy, q], zsem, j, z_dev(q)).wait_recv()

    loop(1, 8, z_recv)
    loop(1, 16, lambda j: remote(hb.at[xy], hb.at[xy], xsem, j, xy_dev((xy + j) % 16)).start())

    table_copy.wait()

    def flip_tile(t):
        tab_t[t] = tab[pl.ds(pl.multiple_of(t * TILE, TILE), TILE), :].astype(F32).T.astype(BF16)

    loop(0, n_tile, flip_tile)
    run[0:1, :] = jnp.full((1, rows), NEGATIVE, F32)
    run[1:3, :] = jnp.zeros((2, rows), F32)
    ght[...] = jnp.zeros(ght.shape, F32)

    def unpack(v):
        for q in range(8):
            piece = hb[v, q].astype(F32)
            n0 = (q // 4) * share + (v // 4) * 128 + (q % 4) * 32 + (v % 4) * 8
            n0 = pl.multiple_of(n0, 8)
            hf[pl.ds(n0, 8), 0:128] = piece[:8]
            hf[pl.ds(n0, 8), 128:256] = piece[8:]

    unpack(xy)

    def x_recv(j):
        v = (xy + 16 - j) % 16
        remote(hb.at[v], hb.at[v], xsem, j, xy_dev(v)).wait_recv()
        unpack(v)

    loop(1, 16, x_recv)
    for c in range(rows // 128):
        ht[:, c * 128:(c + 1) * 128] = hf[c * 128:(c + 1) * 128, :].T.astype(BF16)
    for rel in range(8):
        to = (par + (rel // 2) % 2) % 2 + 2 * ((half + rel % 2) % 2)
        f0 = pl.multiple_of((to * 2 + (k + rel // 4) % 2) * 32, 32)
        hp[rel * 32:(rel + 1) * 32, :] = ht[pl.ds(f0, 32), :]
    meta_copy.wait_send()
    remote(metab.at[1 - half], metab.at[1 - half], msem, 0, other).wait_recv()

    weight = jnp.concatenate([metab[0, 16:17, :], metab[1, 16:17, :]], axis=1)
    aim = jnp.concatenate([metab[0, 17:18, :], metab[1, 17:18, :]], axis=1) - (half * n_half).astype(F32)
    item_at = lax.broadcasted_iota(jnp.int32, (TILE, LANES), 0).astype(F32)

    def score_tile(t):
        items = tab[pl.ds(pl.multiple_of(t * TILE, TILE), TILE), :]
        block = (half * n_tile + t) * TILE // BLK
        bias = jnp.concatenate([metab[0, pl.ds(block, 1), :], metab[1, pl.ds(block, 1), :]], axis=1)
        here = aim - (t * TILE).astype(F32)
        for c in range(rows // LANES):
            at = slice(c * LANES, (c + 1) * LANES)
            s = jnp.dot(items, ht[:, at], preferred_element_type=F32) + bias[:, at]
            top = jnp.max(s, axis=0, keepdims=True)
            e = jnp.exp(s - top)
            pbuf[t, :, at] = e
            total = jnp.sum(e, axis=0, keepdims=True)
            hit = jnp.sum(jnp.where(item_at == here[:, at], s, 0.0), axis=0, keepdims=True)
            mt[t, :, at] = top
            old = run[0:1, at]
            new = jnp.maximum(old, top)
            run[0:1, at] = new
            run[1:2, at] = run[1:2, at] * jnp.exp(old - new) + total * jnp.exp(top - new)
            run[2:3, at] = run[2:3, at] + hit

    loop(0, n_tile, score_tile)

    for part in range(3):
        for c in range(8):
            stx[xy, part * 8 + c:part * 8 + c + 1, :] = run[part:part + 1, c * 128:(c + 1) * 128]
    loop(1, 16, lambda j: remote(stx.at[xy], stx.at[xy], sxsem, j, xy_dev((xy + j) % 16)).start())

    def sx_recv(j):
        v = (xy + 16 - j) % 16
        remote(stx.at[v], stx.at[v], sxsem, j, xy_dev(v)).wait_recv()

    def merge(ref, n):
        top = ref[0, 0:8, :]
        for v in range(1, n):
            top = jnp.maximum(top, ref[v, 0:8, :])
        total = jnp.zeros_like(top)
        hit = jnp.zeros_like(top)
        for v in range(n):
            total = total + ref[v, 8:16, :] * jnp.exp(ref[v, 0:8, :] - top)
            hit = hit + ref[v, 16:24, :]
        return top, total, hit

    loop(1, 16, sx_recv)
    top, total, hit = merge(stx, 16)
    stz[qm, 0:8, :] = top
    stz[qm, 8:16, :] = total
    stz[qm, 16:24, :] = hit
    loop(1, 8, lambda j: remote(stz.at[qm], stz.at[qm], szsem, j, z_dev((qm + j) % 8)).start())

    def sz_recv(j):
        q = (qm + 8 - j) % 8
        remote(stz.at[q], stz.at[q], szsem, j, z_dev(q)).wait_recv()

    loop(1, 8, sz_recv)
    top, total, hit = merge(stz, 8)
    loss[...] = top + jnp.log(total) - hit
    row_top = jnp.concatenate([top[c:c + 1, :] for c in range(8)], axis=1)
    row_total = jnp.concatenate([total[c:c + 1, :] for c in range(8)], axis=1)
    scale = weight / row_total

    def a_step(t):
        remote(a_recv.at[t], a_recv.at[t], asem, t, sibling).wait_recv()
        summed = a_keep[t] + a_recv[t].astype(F32)
        b_send[t] = summed[64:].astype(BF16)
        b_keep[t] = summed[:64]
        remote(b_send.at[t], b_recv.at[t], bsem, t, partner).start()

    def columns(which, t):
        return pl.ds(pl.multiple_of(which * n_half + t * TILE, TILE), TILE)

    def b_step(t):
        remote(b_recv.at[t], b_recv.at[t], bsem, t, partner).wait_recv()
        summed = (b_keep[t] + b_recv[t].astype(F32)).astype(BF16)
        c_send[t] = summed[32:]
        gt_out[:, columns(half, t)] = summed[:32]
        remote(c_send.at[t], gt_out.at[:, columns(half, t)], csem, t, other).start()

    def grad_tile(t):
        here = aim - (t * TILE).astype(F32)
        factor = jnp.exp(mt[t] - row_top) * scale
        for c in range(rows // LANES):
            at = slice(c * LANES, (c + 1) * LANES)
            coef = pbuf[t, :, at] * factor[:, at] - jnp.where(item_at == here[:, at], weight[:, at], 0.0)
            coef = coef.astype(BF16)
            cbuf[:, at] = coef
            ght[:, at] += jnp.dot(tab_t[t], coef, preferred_element_type=F32)
        g = lax.dot_general(hp[...], cbuf[...], (((1,), (1,)), ((), ())), preferred_element_type=F32)
        a_send[t] = g[128:].astype(BF16)
        a_keep[t] = g[:128]
        remote(a_send.at[t], a_recv.at[t], asem, t, sibling).start()

        @pl.when(t >= LAG_CORE)
        def _():
            a_step(t - LAG_CORE)

        @pl.when(t >= LAG_CHIP)
        def _():
            b_step(t - LAG_CHIP)

    loop(0, n_tile, grad_tile)

    for c in range(rows // 128):
        hf[c * 128:(c + 1) * 128, :] = ght[:, c * 128:(c + 1) * 128].T

    def gather_rows(v):
        pieces = []
        for q in range(8):
            n0 = pl.multiple_of((q // 4) * share + (v // 4) * 128 + (q % 4) * 32 + (v % 4) * 8, 8)
            pieces.append(hf[pl.ds(n0, 8), :])
        return jnp.concatenate(pieces, axis=0)

    def g_send(j):
        v = (xy + j) % 16
        gs[v] = gather_rows(v).astype(BF16)
        remote(gs.at[v], gr.at[xy], gxsem, j, xy_dev(v)).start()

    loop(1, 16, g_send)
    mine = gather_rows(xy)
    loop(n_tile - LAG_CORE, n_tile, a_step)

    def gx_recv(j, total):
        v = (xy + 16 - j) % 16
        remote(gr.at[v], gr.at[v], gxsem, j, xy_dev(v)).wait_recv()
        return total + gr[v].astype(F32)

    total = lax.fori_loop(1, 16, gx_recv, mine)
    for q in range(8):
        zs[q] = total[q * 8:(q + 1) * 8, :]
    loop(1, 8, lambda j: remote(zs.at[(qm + j) % 8], zr.at[qm], gzsem, j, z_dev((qm + j) % 8)).start())
    loop(n_tile - LAG_CHIP, n_tile, b_step)

    def gz_recv(j, total):
        q = (qm + 8 - j) % 8
        remote(zr.at[q], zr.at[q], gzsem, j, z_dev(q)).wait_recv()
        return total + zr[q]

    gh_out[...] = lax.fori_loop(1, 8, gz_recv, zs[qm]).astype(BF16)

    def z_sent(j):
        q = (qm + j) % 8
        remote(hb.at[xy, qm], hb.at[xy, qm], zsem, j, z_dev(q)).wait_send()
        remote(stz.at[qm], stz.at[qm], szsem, j, z_dev(q)).wait_send()
        remote(zs.at[q], zr.at[qm], gzsem, j, z_dev(q)).wait_send()

    def x_sent(j):
        v = (xy + j) % 16
        remote(hb.at[xy], hb.at[xy], xsem, j, xy_dev(v)).wait_send()
        remote(stx.at[xy], stx.at[xy], sxsem, j, xy_dev(v)).wait_send()
        remote(gs.at[v], gr.at[xy], gxsem, j, xy_dev(v)).wait_send()

    def t_sent(t):
        remote(a_send.at[t], a_recv.at[t], asem, t, sibling).wait_send()
        remote(b_send.at[t], b_recv.at[t], bsem, t, partner).wait_send()
        remote(c_send.at[t], gt_out.at[:, columns(half, t)], csem, t, other).wait_send()
        into = gt_out.at[:, columns(1 - half, t)]
        remote(c_send.at[t], into, csem, t, other).wait_recv()

    loop(1, 8, z_sent)
    loop(1, 16, x_sent)
    loop(0, n_tile, t_sent)


def on_device(hidden, item_table, bucket_blocks, targets, row_weight):
    i = lax.axis_index("item")
    half = lax.axis_index("batch") // 4
    items, feat = item_table.shape
    share = targets.shape[0]
    n_half = items // 2
    n_tile = n_half // TILE
    rows = 2 * share
    blocks = items // BLK
    local = bucket_blocks - i * blocks
    listed = jnp.any(local[None, :, :] == jnp.arange(16, dtype=jnp.int32)[:, None, None], axis=2)
    bias = jnp.where(listed, 0.0, NEGATIVE).astype(F32)
    bias = jnp.repeat(bias, share // bias.shape[1], axis=1)
    aim = (targets - i * items).astype(F32)
    meta = jnp.concatenate([bias, row_weight[None], aim[None], jnp.zeros((6, share), F32)], axis=0)

    vmem = pltpu.VMEM
    dma = pltpu.SemaphoreType.DMA
    scratch = [
        vmem((n_half, feat), BF16),
        vmem((n_tile, feat, TILE), BF16),
        vmem((16, 8, 16, 128), BF16),
        vmem((rows, feat), F32),
        vmem((feat, rows), BF16),
        vmem((feat, rows), BF16),
        vmem((2, 24, share), F32),
        vmem((n_tile, TILE, rows), F32),
        vmem((n_tile, 1, rows), F32),
        vmem((8, rows), F32),
        vmem((16, 24, 128), F32),
        vmem((8, 24, 128), F32),
        vmem((TILE, rows), BF16),
        vmem((feat, rows), F32),
        vmem((16, 64, feat), BF16),
        vmem((16, 64, feat), BF16),
        vmem((8, 8, feat), F32),
        vmem((8, 8, feat), F32),
        vmem((n_tile, 128, TILE), BF16),
        vmem((n_tile, 128, TILE), F32),
        vmem((n_tile, 128, TILE), BF16),
        vmem((n_tile, 64, TILE), BF16),
        vmem((n_tile, 64, TILE), F32),
        vmem((n_tile, 64, TILE), BF16),
        vmem((n_tile, 32, TILE), BF16),
        dma,
        dma((2, 1)),
        dma((2, 8)),
        dma((2, 16)),
        dma((2, 16)),
        dma((2, 8)),
        dma((2, n_tile)),
        dma((2, n_tile)),
        dma((2, n_tile)),
        dma((2, 16)),
        dma((2, 8)),
    ]
    in_vmem = pl.BlockSpec(memory_space=pltpu.VMEM)
    loss, gh, gt = pl.pallas_call(
        kernel,
        out_shape=(
            jax.ShapeDtypeStruct((8, 128), F32),
            jax.ShapeDtypeStruct(hidden.shape, BF16),
            jax.ShapeDtypeStruct((feat // 8, items), BF16),
        ),
        in_specs=[in_vmem, in_vmem, pl.BlockSpec(memory_space=pl.ANY)],
        out_specs=(in_vmem, in_vmem, in_vmem),
        scratch_shapes=scratch,
        compiler_params=pltpu.CompilerParams(
            collective_id=0, has_side_effects=True, vmem_limit_bytes=56 * 2**20),
    )(hidden, meta, item_table)
    own = lax.dynamic_slice_in_dim(loss.reshape(-1), half * share + i * hidden.shape[0], hidden.shape[0])
    return own, gh, gt


def solution(mesh):
    in_specs = (
        P(("batch", "item"), None),
        P("item", None),
        P("batch", None),
        P("batch"),
        P("batch"),
    )
    out_specs = (P(("batch", "item")), P(("batch", "item"), None), P("batch", "item"))
    return jax.shard_map(on_device, mesh=mesh, in_specs=in_specs, out_specs=out_specs, check_vma=False)
```

```python
import jax
import jax.numpy as jnp
from jax import lax
from jax.experimental import pallas as pl
from jax.experimental.pallas import tpu as pltpu
from jax.sharding import PartitionSpec as P

MESH = pl.DeviceIdType.MESH
F32 = jnp.float32
BF16 = jnp.bfloat16

BLK = 512
NEGATIVE = -1e30
TILE = 256
GROUP = 3
LAG_CORE = 2
LAG_CHIP = 5
EARLY = 2
REACH = (0, 1, 7, 2, 6, 3, 5, 4)
PIECES = ((0, 1), (1, 3), (3, 5), (5, 7), (7, 8))


def kernel(hid_hbm, lists_hbm, targets_hbm, weights_hbm, table, loss, gh_out, gt_out,
           hid, lists, targets, weights, tab, tab_t, hb, hf, ht, hp, metab, bias, pbuf, mt, stx, stz, cbuf, obuf, ut, vt, gs, gr, zs, zr,
           a_send, a_keep, a_recv, b_send, b_keep, b_recv, c_send,
           tsem, insem, msem, zsem, xsem, sxsem, szsem, hxsem, hzsem, asem, bsem, csem, gxsem, gzsem):
    b = lax.axis_index("batch")
    i = lax.axis_index("item")
    zl, k = b // 2, b % 2
    par, half = zl % 2, zl // 2
    x, zh, y = i // 16, (i // 4) % 4, i % 4
    xy = x * 4 + y
    qm = zh * 2 + half
    n_half = tab.shape[0]
    n_tile = n_half // TILE
    n_group = n_tile // GROUP

    def z_dev(q):
        return ((par + 2 * (q % 2)) * 2 + k, x * 16 + (q // 2) * 4 + y)

    def xy_dev(v):
        return (b, (v // 4) * 16 + zh * 4 + v % 4)

    sibling = (zl * 2 + 1 - k, i)
    partner = ((zl + 1 - 2 * par) * 2 + k, i)
    other = ((par + 2 * (1 - half)) * 2 + k, i)

    def remote(src, dst, sems, j, dev):
        return pltpu.make_async_remote_copy(
            src_ref=src, dst_ref=dst, send_sem=sems.at[0, j], recv_sem=sems.at[1, j],
            device_id=dev, device_id_type=MESH)

    def loop(lo, hi, body):
        def step(j, carry):
            body(j)
            return carry
        lax.fori_loop(lo, hi, step, 0)

    table_copy = pltpu.make_async_copy(table.at[pl.ds(half * n_half, n_half), :], tab, tsem)
    table_copy.start()
    inputs = [
        pltpu.make_async_copy(src, dst, insem.at[n])
        for n, (src, dst) in enumerate(
            ((hid_hbm, hid), (lists_hbm, lists), (targets_hbm, targets), (weights_hbm, weights)))
    ]
    for copy in inputs:
        copy.start()

    barrier = pltpu.get_barrier_semaphore()

    def greet(dev):
        pl.semaphore_signal(barrier, inc=1, device_id=dev, device_id_type=MESH)

    for j in (4, 3, 5, 2, 6, 1, 7):
        greet(z_dev((qm + j) % 8))
    loop(1, 16, lambda j: greet(xy_dev((xy + j) % 16)))
    greet(sibling)
    greet(partner)

    for copy in inputs:
        copy.wait()
    own = hid[...].astype(F32)
    hb[xy, 0] = jnp.concatenate([own[:, :128], own[:, 128:]], axis=0).astype(BF16)
    metab[half, 0:8, :] = lists[...].astype(F32)
    lane = lax.broadcasted_iota(jnp.int32, (1, 128), 1)
    for at, ref in ((8, targets), (12, weights)):
        rows = ref[...].astype(F32)
        turned = [rows if d == 0 else pltpu.roll(rows, 32 * d, 1) for d in range(4)]
        for to in range(4):
            line = jnp.zeros((1, 128), F32)
            for fx in range(4):
                line = jnp.where(lane // 32 == fx, turned[(fx - to) % 4][fx:fx + 1, :], line)
            metab[half, at + to:at + to + 1, :] = line
    pl.semaphore_wait(barrier, 24)

    for j in (4, 3, 5, 2, 6, 1, 7):
        remote(hb.at[xy, 0], hb.at[xy, REACH.index(8 - j)], zsem, 8 - j, z_dev((qm + j) % 8)).start()
    meta_copy = remote(metab.at[half], metab.at[half], msem, 0, other)
    meta_copy.start()

    def x_copy(piece, v_from, v_to, j):
        lo, hi = PIECES[piece]
        ref = hb.at[v_from, lo:hi]
        return remote(ref, ref, xsem, piece * 16 + j, xy_dev(v_to))

    def x_send(piece):
        loop(1, 16, lambda j: x_copy(piece, xy, (xy + j) % 16, j).start())

    def z_recv(piece):
        for s in range(*PIECES[piece]):
            q = (qm + REACH[s]) % 8
            remote(hb.at[xy, s], hb.at[xy, s], zsem, REACH[s], z_dev(q)).wait_recv()

    x_send(0)
    table_copy.wait()

    def flip_group(g):
        part = tab[pl.ds(pl.multiple_of(g * GROUP * TILE, TILE), GROUP * TILE), :]
        tab_t[g] = part.astype(F32).T.astype(BF16)

    loop(0, 1, flip_group)
    z_recv(1)
    x_send(1)
    loop(1, 2, flip_group)
    z_recv(2)
    x_send(2)
    loop(2, 3, flip_group)

    meta_copy.wait_send()
    remote(metab.at[1 - half], metab.at[1 - half], msem, 0, other).wait_recv()
    base = (i * 2 * n_half // BLK + half * (n_tile * TILE // BLK)).astype(F32)
    bucket = lax.broadcasted_iota(jnp.int32, (8, 128), 0)
    column = lax.broadcasted_iota(jnp.int32, (8, 128), 1) // 32
    for g in range(2):
        local = metab[g, 0:8, :] - base
        for blk in range(8):
            listed = jnp.max(jnp.where(local == blk, 1.0, 0.0), axis=1, keepdims=True)
            for side in range(2):
                spread = jnp.where(bucket == column * 2 + side, listed, 0.0)
                line = jnp.max(spread, axis=0, keepdims=True)
                bias[g * 2 + side, blk:blk + 1, :] = jnp.where(line > 0.0, 0.0, NEGATIVE)

    aim_base = (i * 2 * n_half + half * n_half).astype(F32)
    aims, weight = [], []
    for q in range(8):
        aims.append(metab[q % 2, 8 + q // 2:9 + q // 2, :] - aim_base)
        weight.append(metab[q % 2, 12 + q // 2:13 + q // 2, :])
    aim = jnp.concatenate(aims, axis=0)
    weight = jnp.concatenate(weight, axis=0)
    item_at = lax.broadcasted_iota(jnp.int32, (TILE, 128), 0).astype(F32)

    def unpack(piece, v):
        for s in range(*PIECES[piece]):
            part = hb[v, s].astype(F32)
            rows = pl.ds(pl.multiple_of(v * 8, 8), 8)
            hf[s, rows, 0:128] = part[:8]
            hf[s, rows, 128:256] = part[8:]

    def score(piece):
        def x_recv(j):
            v = (xy + 16 - j) % 16
            x_copy(piece, v, v, j).wait_recv()
            unpack(piece, v)

        unpack(piece, xy)
        loop(1, 16, x_recv)
        places = []
        for s in range(*PIECES[piece]):
            q = (qm + REACH[s]) % 8
            ht[q] = hf[s].T.astype(BF16)
            q_aim = metab[q % 2, pl.ds(8 + q // 2, 1), :] - aim_base
            places.append((q, (q % 2) * 2 + q // 4, q_aim))

        def score_group(g, carry):
            carry = list(carry)
            for u in range(GROUP):
                t = g * GROUP + u
                items = tab[pl.ds(pl.multiple_of(t * TILE, TILE), TILE), :]
                for at, (q, side, q_aim) in enumerate(places):
                    old, total, hit = carry[at]
                    s = jnp.dot(items, ht[q], preferred_element_type=F32)
                    top = jnp.max(s, axis=0, keepdims=True)
                    e = jnp.exp(s - top)
                    pbuf[q, t] = e
                    top = top + bias[side, pl.ds((t + half) // 2, 1), :]
                    mt[t, pl.ds(q, 1), :] = top
                    new = jnp.maximum(old, top)
                    total = total * jnp.exp(old - new) + jnp.sum(e, axis=0, keepdims=True) * jnp.exp(top - new)
                    here = q_aim - (t * TILE).astype(F32)
                    hit = hit + jnp.sum(jnp.where(item_at == here, s, 0.0), axis=0, keepdims=True)
                    carry[at] = (new, total, hit)
            return tuple(carry)

        zero = jnp.zeros((1, 128), F32)
        done = lax.fori_loop(0, n_group, score_group, tuple((zero + NEGATIVE, zero, zero) for _ in places))
        for (q, _, _), (top, total, hit) in zip(places, done):
            stx[xy, pl.ds(q, 1), :] = top
            stx[xy, pl.ds(8 + q, 1), :] = total
            stx[xy, pl.ds(16 + q, 1), :] = hit

    score(0)
    z_recv(3)
    x_send(3)
    z_recv(4)
    x_send(4)
    loop(3, n_group, flip_group)
    for piece in range(1, 5):
        score(piece)

    def sx_copy(hits, j, v_from, v_to):
        ref = stx.at[v_from, 16:24] if hits else stx.at[v_from, 0:16]
        return remote(ref, ref, hxsem if hits else sxsem, j, xy_dev(v_to))

    def sz_copy(hits, j, q_from, q_to):
        ref = stz.at[q_from, 16:24] if hits else stz.at[q_from, 0:16]
        return remote(ref, ref, hzsem if hits else szsem, j, z_dev(q_to))

    loop(1, 16, lambda j: sx_copy(False, j, xy, (xy + j) % 16).start())
    loop(1, 16, lambda j: sx_copy(True, j, xy, (xy + j) % 16).start())
    top_here = stx[xy, 0:8, :]
    hit_here = stx[xy, 16:24, :]

    for rel in range(8):
        to = (par + (rel // 2) % 2) % 2 + 2 * ((half + rel % 2) % 2)
        f0 = pl.multiple_of((to * 2 + (k + rel // 4) % 2) * 32, 32)
        for q in range(8):
            hp[rel * 32:(rel + 1) * 32, q * 128:(q + 1) * 128] = ht[q, pl.ds(f0, 32), :]

    ut[...] = jnp.zeros(ut.shape, F32)
    vt[...] = jnp.zeros(vt.shape, F32)

    def early_group(g):
        for u in range(GROUP):
            t = g * GROUP + u
            here = aim - (t * TILE).astype(F32)
            factor = jnp.exp(mt[t] - top_here)
            for q in range(8):
                at = slice(q * 128, (q + 1) * 128)
                aimed = item_at == here[q:q + 1, :]
                cbuf[u * TILE:(u + 1) * TILE, at] = jnp.where(aimed, 0.0, pbuf[q, t] * factor[q:q + 1, :]).astype(BF16)
                obuf[u * TILE:(u + 1) * TILE, at] = jnp.where(aimed, 1.0, 0.0).astype(BF16)
        ut[...] += jnp.dot(tab_t[g], cbuf[...], preferred_element_type=F32)
        vt[...] += jnp.dot(tab_t[g], obuf[...], preferred_element_type=F32)

    loop(0, EARLY, early_group)

    def merge(ref, n):
        top = ref[0, 0:8, :]
        for v in range(1, n):
            top = jnp.maximum(top, ref[v, 0:8, :])
        total = jnp.zeros_like(top)
        for v in range(n):
            total = total + ref[v, 8:16, :] * jnp.exp(ref[v, 0:8, :] - top)
        return top, total

    def sum_hits(ref, n):
        hit = ref[0, 16:24, :]
        for v in range(1, n):
            hit = hit + ref[v, 16:24, :]
        return hit

    def sx_wait(hits):
        def wait(j):
            v = (xy + 16 - j) % 16
            sx_copy(hits, j, v, v).wait_recv()
        loop(1, 16, wait)

    def sz_wait(hits):
        for j in range(1, 8):
            q = (qm + 8 - j) % 8
            sz_copy(hits, j, q, q).wait_recv()

    sx_wait(False)
    top, total = merge(stx, 16)
    stz[qm, 0:8, :] = top
    stz[qm, 8:16, :] = total
    for j in (4, 3, 5, 2, 6, 1, 7):
        sz_copy(False, j, qm, (qm + j) % 8).start()
    sx_wait(True)
    stz[qm, 16:24, :] = sum_hits(stx, 16)
    for j in (4, 3, 5, 2, 6, 1, 7):
        sz_copy(True, j, qm, (qm + j) % 8).start()
    loop(EARLY, n_group, early_group)
    sz_wait(False)
    top, total = merge(stz, 8)
    scale = weight / total

    def a_step(t):
        remote(a_recv.at[t], a_recv.at[t], asem, t, sibling).wait_recv()
        summed = a_keep[t] + a_recv[t].astype(F32)
        b_send[t] = summed[64:].astype(BF16)
        b_keep[t] = summed[:64]
        remote(b_send.at[t], b_recv.at[t], bsem, t, partner).start()

    def columns(which, t):
        return pl.ds(pl.multiple_of(which * n_half + t * TILE, TILE), TILE)

    def b_step(t):
        remote(b_recv.at[t], b_recv.at[t], bsem, t, partner).wait_recv()
        summed = (b_keep[t] + b_recv[t].astype(F32)).astype(BF16)
        c_send[t] = summed[32:]
        gt_out[:, columns(half, t)] = summed[:32]
        remote(c_send.at[t], gt_out.at[:, columns(half, t)], csem, t, other).start()

    def grad_tile(t):
        here = aim - (t * TILE).astype(F32)
        factor = jnp.exp(mt[t] - top) * scale
        for q in range(8):
            at = slice(q * 128, (q + 1) * 128)
            less = jnp.where(item_at == here[q:q + 1, :], weight[q:q + 1, :], 0.0)
            cbuf[0:TILE, at] = (pbuf[q, t] * factor[q:q + 1, :] - less).astype(BF16)
        g = lax.dot_general(hp[...], cbuf[0:TILE, :], (((1,), (1,)), ((), ())), preferred_element_type=F32)
        a_send[t] = g[128:].astype(BF16)
        a_keep[t] = g[:128]
        remote(a_send.at[t], a_recv.at[t], asem, t, sibling).start()

        @pl.when(t >= LAG_CORE)
        def _():
            a_step(t - LAG_CORE)

        @pl.when(t >= LAG_CHIP)
        def _():
            b_step(t - LAG_CHIP)

    loop(0, LAG_CORE, grad_tile)

    on_here = (aim >= 0.0) & (aim < float(n_half))
    chance = jnp.exp(jnp.where(on_here, hit_here, NEGATIVE) - top) / total
    of_target = weight * (chance - 1.0)
    of_rest = jnp.exp(top_here - top) * scale
    for q in range(8):
        at = slice(q * 128, (q + 1) * 128)
        grad = ut[:, at] * of_rest[q:q + 1, :] + vt[:, at] * of_target[q:q + 1, :]
        hf[q] = grad.T

    def gather_rows(v):
        rows = pl.ds(pl.multiple_of(v * 8, 8), 8)
        return jnp.concatenate([hf[q, rows, :] for q in range(8)], axis=0)

    def g_send(j):
        v = (xy + j) % 16
        gs[v] = gather_rows(v).astype(BF16)
        remote(gs.at[v], gr.at[xy], gxsem, j, xy_dev(v)).start()

    loop(1, 16, g_send)
    mine = gather_rows(xy)
    loop(LAG_CORE, n_tile, grad_tile)
    loop(n_tile - LAG_CORE, n_tile, a_step)

    def gx_recv(j, total):
        v = (xy + 16 - j) % 16
        remote(gr.at[v], gr.at[v], gxsem, j, xy_dev(v)).wait_recv()
        return total + gr[v].astype(F32)

    summed = lax.fori_loop(1, 16, gx_recv, mine)
    for q in range(8):
        zs[q] = summed[q * 8:(q + 1) * 8, :]
    for j in (4, 3, 5, 2, 6, 1, 7):
        remote(zs.at[(qm + j) % 8], zr.at[qm], gzsem, j, z_dev((qm + j) % 8)).start()
    loop(n_tile - LAG_CHIP, n_tile, b_step)

    sz_wait(True)
    loss_all = top + jnp.log(total) - sum_hits(stz, 8)
    bucket_is_own = bucket == qm
    line = jnp.sum(jnp.where(bucket_is_own, loss_all, 0.0), axis=0, keepdims=True)
    loss[...] = pltpu.roll(jnp.broadcast_to(line, (8, 128)), (128 - xy * 8) % 128, 1)

    grad = zs[qm]
    for j in range(1, 8):
        q = (qm + 8 - j) % 8
        remote(zr.at[q], zr.at[q], gzsem, j, z_dev(q)).wait_recv()
        grad = grad + zr[q]
    gh_out[...] = grad.astype(BF16)

    for j in range(1, 8):
        q = (qm + j) % 8
        remote(hb.at[xy, 0], hb.at[xy, REACH.index(8 - j)], zsem, 8 - j, z_dev(q)).wait_send()
        sz_copy(False, j, qm, q).wait_send()
        sz_copy(True, j, qm, q).wait_send()
        remote(zs.at[q], zr.at[qm], gzsem, j, z_dev(q)).wait_send()

    def x_sent(j):
        v = (xy + j) % 16
        for piece in range(5):
            x_copy(piece, xy, v, j).wait_send()
        sx_copy(False, j, xy, v).wait_send()
        sx_copy(True, j, xy, v).wait_send()
        remote(gs.at[v], gr.at[xy], gxsem, j, xy_dev(v)).wait_send()

    def t_sent(t):
        remote(a_send.at[t], a_recv.at[t], asem, t, sibling).wait_send()
        remote(b_send.at[t], b_recv.at[t], bsem, t, partner).wait_send()
        remote(c_send.at[t], gt_out.at[:, columns(half, t)], csem, t, other).wait_send()
        into = gt_out.at[:, columns(1 - half, t)]
        remote(c_send.at[t], into, csem, t, other).wait_recv()

    loop(1, 16, x_sent)
    loop(0, n_tile, t_sent)


def finish(loss, gh, gt, loss_out, gh_out, gt_out, sem):
    copies = [pltpu.make_async_copy(gt, gt_out, sem.at[0]), pltpu.make_async_copy(gh, gh_out, sem.at[1])]
    for c in copies:
        c.start()
    for r in range(loss_out.shape[0]):
        loss_out[r] = loss[0, r]
    for c in copies:
        c.wait()


def on_device(hidden, item_table, bucket_blocks, targets, row_weight):
    items, feat = item_table.shape
    n_half = items // 2
    n_tile = n_half // TILE
    n_group = n_tile // GROUP
    rows = 8 * 128

    vmem = pltpu.VMEM
    dma = pltpu.SemaphoreType.DMA
    scratch = [
        vmem(hidden.shape, BF16),
        vmem(bucket_blocks.shape, jnp.int32),
        vmem((4, 128), jnp.int32),
        vmem((4, 128), F32),
        vmem((n_half, feat), BF16),
        vmem((n_group, feat, GROUP * TILE), BF16),
        vmem((16, 8, 16, 128), BF16),
        vmem((8, 128, feat), F32),
        vmem((8, feat, 128), BF16),
        vmem((feat, rows), BF16),
        vmem((2, 16, 128), F32),
        vmem((4, 8, 128), F32),
        vmem((8, n_tile, TILE, 128), F32),
        vmem((n_tile, 8, 128), F32),
        vmem((16, 24, 128), F32),
        vmem((8, 24, 128), F32),
        vmem((GROUP * TILE, rows), BF16),
        vmem((GROUP * TILE, rows), BF16),
        vmem((feat, rows), F32),
        vmem((feat, rows), F32),
        vmem((16, 64, feat), BF16),
        vmem((16, 64, feat), BF16),
        vmem((8, 8, feat), F32),
        vmem((8, 8, feat), F32),
        vmem((n_tile, 128, TILE), BF16),
        vmem((n_tile, 128, TILE), F32),
        vmem((n_tile, 128, TILE), BF16),
        vmem((n_tile, 64, TILE), BF16),
        vmem((n_tile, 64, TILE), F32),
        vmem((n_tile, 64, TILE), BF16),
        vmem((n_tile, 32, TILE), BF16),
        dma,
        dma((4,)),
        dma((2, 1)),
        dma((2, 8)),
        dma((2, 80)),
        dma((2, 16)),
        dma((2, 8)),
        dma((2, 16)),
        dma((2, 8)),
        dma((2, n_tile)),
        dma((2, n_tile)),
        dma((2, n_tile)),
        dma((2, 16)),
        dma((2, 8)),
    ]
    in_vmem = pl.BlockSpec(memory_space=pltpu.VMEM)
    in_smem = pl.BlockSpec(memory_space=pltpu.SMEM)
    anywhere = pl.BlockSpec(memory_space=pl.ANY)
    gh_shape = jax.ShapeDtypeStruct(hidden.shape, BF16)
    gt_shape = jax.ShapeDtypeStruct((feat // 8, items), BF16)
    loss, gh, gt = pl.pallas_call(
        kernel,
        out_shape=(jax.ShapeDtypeStruct((8, 128), F32), gh_shape, gt_shape),
        in_specs=[pl.BlockSpec(memory_space=pltpu.HBM)] * 5,
        out_specs=(in_vmem, in_vmem, in_vmem),
        scratch_shapes=scratch,
        compiler_params=pltpu.CompilerParams(
            collective_id=0, has_side_effects=True, vmem_limit_bytes=56 * 2**20),
    )(hidden, bucket_blocks, targets.reshape(4, 128), row_weight.reshape(4, 128), item_table)
    return pl.pallas_call(
        finish,
        out_shape=(jax.ShapeDtypeStruct((hidden.shape[0],), F32), gh_shape, gt_shape),
        in_specs=[in_smem, in_vmem, in_vmem],
        out_specs=(in_smem, anywhere, anywhere),
        scratch_shapes=[dma((2,))],
    )(loss, gh, gt)


def solution(mesh):
    in_specs = (
        P(("batch", "item"), None),
        P("item", None),
        P("batch", None),
        P("batch"),
        P("batch"),
    )
    out_specs = (P(("batch", "item")), P(("batch", "item"), None), P("batch", "item"))
    return jax.shard_map(on_device, mesh=mesh, in_specs=in_specs, out_specs=out_specs, check_vma=False)
```

```python
import functools

import jax
import jax.numpy as jnp
from jax import lax
from jax.experimental import pallas as pl
from jax.experimental.pallas import tpu as pltpu
from jax.sharding import PartitionSpec as P

MESH = pl.DeviceIdType.MESH
F32 = jnp.float32
BF16 = jnp.bfloat16

BLK = 512
NEGATIVE = -1e30
TILE = 256
GROUP = 3
LAG_CORE = 4
LAG_CHIP = 9
HIDDEN_AT = 2
EARLY = 2
REACH = (0, 1, 7, 2, 6, 3, 5, 4)
PIECES = ((0, 3), (3, 5), (5, 8))


def kernel(hid_hbm, lists_hbm, targets_hbm, weights_hbm, table, loss, gh_out, gt_out,
           hid, lists, targets, weights, tab, tab_t, hb, hf, ht, hw, hp, metab, bias, pbuf, mt, stx, stz, cbuf, obuf, ut, vt, gs, gr, zs, zk, zr,
           a_send, a_keep, a_recv, b_send, b_keep, b_recv, c_send,
           tsem, insem, msem, zsem, xsem, sxsem, szsem, hxsem, hzsem, asem, bsem, csem, gxsem, gzsem):
    b = lax.axis_index("batch")
    i = lax.axis_index("item")
    zl, k = b // 2, b % 2
    par, half = zl % 2, zl // 2
    x, zh, y = i // 16, (i // 4) % 4, i % 4
    xy = x * 4 + y
    qm = zh * 2 + half
    n_half = tab.shape[0]
    n_tile = n_half // TILE
    n_group = n_tile // GROUP

    def z_dev(q):
        return ((par + 2 * (q % 2)) * 2 + k, x * 16 + (q // 2) * 4 + y)

    def xy_dev(v):
        return (b, (v // 4) * 16 + zh * 4 + v % 4)

    sibling = (zl * 2 + 1 - k, i)
    partner = ((zl + 1 - 2 * par) * 2 + k, i)
    other = ((par + 2 * (1 - half)) * 2 + k, i)

    def remote(src, dst, sems, j, dev):
        return pltpu.make_async_remote_copy(
            src_ref=src, dst_ref=dst, send_sem=sems.at[0, j], recv_sem=sems.at[1, j],
            device_id=dev, device_id_type=MESH)

    def loop(lo, hi, body):
        def step(j, carry):
            body(j)
            return carry
        lax.fori_loop(lo, hi, step, 0)

    table_copy = pltpu.make_async_copy(table.at[pl.ds(half * n_half, n_half), :], tab, tsem)
    table_copy.start()
    inputs = [
        pltpu.make_async_copy(src, dst, insem.at[n])
        for n, (src, dst) in enumerate(
            ((hid_hbm, hid), (lists_hbm, lists), (targets_hbm, targets), (weights_hbm, weights)))
    ]
    for copy in inputs:
        copy.start()

    barrier = pltpu.get_barrier_semaphore()

    def greet(dev):
        pl.semaphore_signal(barrier, inc=1, device_id=dev, device_id_type=MESH)

    for j in (4, 3, 5, 2, 6, 1, 7):
        greet(z_dev((qm + j) % 8))
    loop(1, 16, lambda j: greet(xy_dev((xy + j) % 16)))
    greet(sibling)
    greet(partner)

    for copy in inputs:
        copy.wait()
    own = hid[...].astype(F32)
    hb[xy, 0] = jnp.concatenate([own[:, :128], own[:, 128:]], axis=0).astype(BF16)
    metab[half, 0:8, :] = lists[...].astype(F32)
    lane = lax.broadcasted_iota(jnp.int32, (1, 128), 1)
    for at, ref in ((8, targets), (12, weights)):
        rows = ref[...].astype(F32)
        turned = [rows if d == 0 else pltpu.roll(rows, 32 * d, 1) for d in range(4)]
        for to in range(4):
            line = jnp.zeros((1, 128), F32)
            for fx in range(4):
                line = jnp.where(lane // 32 == fx, turned[(fx - to) % 4][fx:fx + 1, :], line)
            metab[half, at + to:at + to + 1, :] = line
    table_copy.wait()

    def flip_group(g):
        part = tab[pl.ds(pl.multiple_of(g * GROUP * TILE, TILE), GROUP * TILE), :]
        tab_t[g] = part.astype(F32).T.astype(BF16)

    loop(0, n_group, flip_group)
    pl.semaphore_wait(barrier, 24)

    for j in (4, 3, 5, 2, 6, 1, 7):
        remote(hb.at[xy, 0], hb.at[xy, REACH.index(8 - j)], zsem, 8 - j, z_dev((qm + j) % 8)).start()
    meta_copy = remote(metab.at[half], metab.at[half], msem, 0, other)
    meta_copy.start()

    def x_copy(piece, v_from, v_to, j):
        lo, hi = PIECES[piece]
        ref = hb.at[v_from, lo:hi]
        return remote(ref, ref, xsem, piece * 16 + j, xy_dev(v_to))

    def x_send(piece):
        loop(1, 16, lambda j: x_copy(piece, xy, (xy + j) % 16, j).start())

    def z_recv(piece):
        for s in range(*PIECES[piece]):
            if s > 0:
                q = (qm + REACH[s]) % 8
                remote(hb.at[xy, s], hb.at[xy, s], zsem, REACH[s], z_dev(q)).wait_recv()

    z_recv(0)
    x_send(0)

    meta_copy.wait_send()
    remote(metab.at[1 - half], metab.at[1 - half], msem, 0, other).wait_recv()
    base = (i * 2 * n_half // BLK + half * (n_tile * TILE // BLK)).astype(F32)
    bucket = lax.broadcasted_iota(jnp.int32, (8, 128), 0)
    column = lax.broadcasted_iota(jnp.int32, (8, 128), 1) // 32
    for g in range(2):
        local = metab[g, 0:8, :] - base
        for blk in range(8):
            listed = jnp.max(jnp.where(local == blk, 1.0, 0.0), axis=1, keepdims=True)
            for side in range(2):
                spread = jnp.where(bucket == column * 2 + side, listed, 0.0)
                line = jnp.max(spread, axis=0, keepdims=True)
                bias[g * 2 + side, blk:blk + 1, :] = jnp.where(line > 0.0, 0.0, NEGATIVE)

    aim_base = (i * 2 * n_half + half * n_half).astype(F32)
    aims, weight = [], []
    for q in range(8):
        aims.append(metab[q % 2, 8 + q // 2:9 + q // 2, :] - aim_base)
        weight.append(metab[q % 2, 12 + q // 2:13 + q // 2, :])
    aim = jnp.concatenate(aims, axis=0)
    weight = jnp.concatenate(weight, axis=0)
    item_at = lax.broadcasted_iota(jnp.int32, (TILE, 128), 0).astype(F32)

    vt[...] = jnp.zeros(vt.shape, F32)

    def aim_group(g):
        for u in range(GROUP):
            here = aim - ((g * GROUP + u) * TILE).astype(F32)
            for q in range(8):
                aimed = item_at == here[q:q + 1, :]
                obuf[u * TILE:(u + 1) * TILE, q * 128:(q + 1) * 128] = jnp.where(aimed, 1.0, 0.0).astype(BF16)
        vt[...] += jnp.dot(tab_t[g], obuf[...], preferred_element_type=F32)

    for piece in range(1, len(PIECES)):
        loop(2 * piece - 2, min(2 * piece, n_group), aim_group)
        z_recv(piece)
        x_send(piece)
    loop(min(2 * len(PIECES) - 2, n_group), n_group, aim_group)

    def unpack(piece, v):
        for s in range(*PIECES[piece]):
            part = hb[v, s].astype(F32)
            rows = pl.ds(pl.multiple_of(v * 8, 8), 8)
            hf[s, rows, 0:128] = part[:8]
            hf[s, rows, 128:256] = part[8:]

    def score(piece):
        def x_recv(j):
            v = (xy + 16 - j) % 16
            x_copy(piece, v, v, j).wait_recv()
            unpack(piece, v)

        unpack(piece, xy)
        loop(1, 16, x_recv)
        places = []
        for s in range(*PIECES[piece]):
            q = (qm + REACH[s]) % 8
            flat = hf[s].T.astype(BF16)
            ht[q] = flat
            hw[:, len(places) * 128:(len(places) + 1) * 128] = flat
            places.append((q, (q % 2) * 2 + q // 4))
        scores = jnp.dot(tab[...], hw[:, 0:len(places) * 128], preferred_element_type=F32)
        tops = [[] for _ in places]
        sums = [[] for _ in places]
        for t in range(n_tile):
            for at, (q, side) in enumerate(places):
                s = scores[t * TILE:(t + 1) * TILE, at * 128:(at + 1) * 128]
                top = jnp.max(s, axis=0, keepdims=True)
                e = jnp.exp(s - top)
                pbuf[q, t] = e
                top = top + bias[side, pl.ds((t + half) // 2, 1), :]
                mt[t, pl.ds(q, 1), :] = top
                tops[at].append(top)
                sums[at].append(jnp.sum(e, axis=0, keepdims=True))
        for at, (q, side) in enumerate(places):
            top = functools.reduce(jnp.maximum, tops[at])
            stx[xy, pl.ds(q, 1), :] = top
            stx[xy, pl.ds(8 + q, 1), :] = sum(n * jnp.exp(m - top) for n, m in zip(sums[at], tops[at]))

    for piece in range(len(PIECES)):
        score(piece)

    def sx_copy(hits, j, v_from, v_to):
        ref = stx.at[v_from, 16:24] if hits else stx.at[v_from, 0:16]
        return remote(ref, ref, hxsem if hits else sxsem, j, xy_dev(v_to))

    def sz_copy(hits, j, q_from, q_to):
        ref = stz.at[q_from, 16:24] if hits else stz.at[q_from, 0:16]
        return remote(ref, ref, hzsem if hits else szsem, j, z_dev(q_to))

    loop(1, 16, lambda j: sx_copy(False, j, xy, (xy + j) % 16).start())
    top_here = stx[xy, 0:8, :]
    for q in range(8):
        at = slice(q * 128, (q + 1) * 128)
        stx[xy, 16 + q:17 + q, :] = jnp.sum(ht[q].astype(F32) * vt[:, at], axis=0, keepdims=True)
    hit_here = stx[xy, 16:24, :]
    loop(1, 16, lambda j: sx_copy(True, j, xy, (xy + j) % 16).start())

    for rel in range(8):
        to = (par + (rel // 2) % 2) % 2 + 2 * ((half + rel % 2) % 2)
        f0 = pl.multiple_of((to * 2 + (k + rel // 4) % 2) * 32, 32)
        for q in range(8):
            hp[rel * 32:(rel + 1) * 32, q * 128:(q + 1) * 128] = ht[q, pl.ds(f0, 32), :]

    ut[...] = jnp.zeros(ut.shape, F32)

    def early_group(g):
        for u in range(GROUP):
            t = g * GROUP + u
            here = aim - (t * TILE).astype(F32)
            factor = jnp.exp(mt[t] - top_here)
            for q in range(8):
                at = slice(q * 128, (q + 1) * 128)
                aimed = item_at == here[q:q + 1, :]
                cbuf[u * TILE:(u + 1) * TILE, at] = jnp.where(aimed, 0.0, pbuf[q, t] * factor[q:q + 1, :]).astype(BF16)
        ut[...] += jnp.dot(tab_t[g], cbuf[...], preferred_element_type=F32)

    loop(0, EARLY, early_group)

    def merge(ref, n):
        top = ref[0, 0:8, :]
        for v in range(1, n):
            top = jnp.maximum(top, ref[v, 0:8, :])
        total = jnp.zeros_like(top)
        for v in range(n):
            total = total + ref[v, 8:16, :] * jnp.exp(ref[v, 0:8, :] - top)
        return top, total

    def sum_hits(ref, n):
        hit = ref[0, 16:24, :]
        for v in range(1, n):
            hit = hit + ref[v, 16:24, :]
        return hit

    def sx_wait(hits):
        def wait(j):
            v = (xy + 16 - j) % 16
            sx_copy(hits, j, v, v).wait_recv()
        loop(1, 16, wait)

    def sz_wait(hits):
        for j in range(1, 8):
            q = (qm + 8 - j) % 8
            sz_copy(hits, j, q, q).wait_recv()

    sx_wait(False)
    top, total = merge(stx, 16)
    stz[qm, 0:8, :] = top
    stz[qm, 8:16, :] = total
    for j in (4, 3, 5, 2, 6, 1, 7):
        sz_copy(False, j, qm, (qm + j) % 8).start()
    loop(EARLY, n_group, early_group)
    sx_wait(True)
    stz[qm, 16:24, :] = sum_hits(stx, 16)
    for j in (4, 3, 5, 2, 6, 1, 7):
        sz_copy(True, j, qm, (qm + j) % 8).start()

    def x_sent(j):
        v = (xy + j) % 16
        for piece in range(len(PIECES)):
            x_copy(piece, xy, v, j).wait_send()
        sx_copy(False, j, xy, v).wait_send()
        sx_copy(True, j, xy, v).wait_send()

    loop(1, 16, x_sent)
    for j in range(1, 8):
        q = (qm + j) % 8
        remote(hb.at[xy, 0], hb.at[xy, REACH.index(8 - j)], zsem, 8 - j, z_dev(q)).wait_send()
        sz_copy(False, j, qm, q).wait_send()
        sz_copy(True, j, qm, q).wait_send()
    sz_wait(False)
    top, total = merge(stz, 8)
    scale = weight / total

    def a_step(t):
        remote(a_send.at[t], a_recv.at[t], asem, t, sibling).wait()
        summed = a_keep[t] + a_recv[t].astype(F32)
        b_send[t] = summed[64:].astype(BF16)
        b_keep[t] = summed[:64]
        remote(b_send.at[t], b_recv.at[t], bsem, t, partner).start()

    def columns(which, t):
        return pl.ds(pl.multiple_of(which * n_half + t * TILE, TILE), TILE)

    def b_step(t):
        remote(b_send.at[t], b_recv.at[t], bsem, t, partner).wait()
        summed = (b_keep[t] + b_recv[t].astype(F32)).astype(BF16)
        c_send[t] = summed[32:]
        gt_out[:, columns(half, t)] = summed[:32]
        remote(c_send.at[t], gt_out.at[:, columns(half, t)], csem, t, other).start()

    def grad_tile(t):
        here = aim - (t * TILE).astype(F32)
        factor = jnp.exp(mt[t] - top) * scale
        for q in range(8):
            at = slice(q * 128, (q + 1) * 128)
            less = jnp.where(item_at == here[q:q + 1, :], weight[q:q + 1, :], 0.0)
            cbuf[0:TILE, at] = (pbuf[q, t] * factor[q:q + 1, :] - less).astype(BF16)
        g = lax.dot_general(hp[...], cbuf[0:TILE, :], (((1,), (1,)), ((), ())), preferred_element_type=F32)
        a_send[t] = g[128:].astype(BF16)
        a_keep[t] = g[:128]
        remote(a_send.at[t], a_recv.at[t], asem, t, sibling).start()

        @pl.when(t >= LAG_CORE)
        def _():
            a_step(t - LAG_CORE)

        @pl.when(t >= LAG_CHIP)
        def _():
            b_step(t - LAG_CHIP)

    loop(0, HIDDEN_AT, grad_tile)

    on_here = (aim >= 0.0) & (aim < float(n_half))
    chance = jnp.exp(jnp.where(on_here, hit_here, NEGATIVE) - top) / total
    of_target = weight * (chance - 1.0)
    of_rest = jnp.exp(top_here - top) * scale
    for q in range(8):
        at = slice(q * 128, (q + 1) * 128)
        grad = ut[:, at] * of_rest[q:q + 1, :] + vt[:, at] * of_target[q:q + 1, :]
        hf[q] = grad.T

    def gather_rows(v):
        rows = pl.ds(pl.multiple_of(v * 8, 8), 8)
        return jnp.concatenate([hf[q, rows, :] for q in range(8)], axis=0)

    def g_send(j):
        v = (xy + j) % 16
        gs[v] = gather_rows(v).astype(BF16)
        remote(gs.at[v], gr.at[xy], gxsem, j, xy_dev(v)).start()

    loop(1, 16, g_send)
    mine = gather_rows(xy)
    loop(HIDDEN_AT, n_tile, grad_tile)
    loop(n_tile - LAG_CORE, n_tile, a_step)
    def gx_recv(j, total):
        v = (xy + 16 - j) % 16
        remote(gr.at[v], gr.at[v], gxsem, j, xy_dev(v)).wait_recv()
        to = (xy + j) % 16
        remote(gs.at[to], gr.at[xy], gxsem, j, xy_dev(to)).wait_send()
        return total + gr[v].astype(F32)

    summed = lax.fori_loop(1, 16, gx_recv, mine)
    for q in range(8):
        part = summed[q * 8:(q + 1) * 8, :]
        zs[q] = jnp.concatenate([part[:, :128], part[:, 128:]], axis=0).astype(BF16)
        zk[q] = part
    for j in (4, 3, 5, 2, 6, 1, 7):
        remote(zs.at[(qm + j) % 8], zr.at[qm], gzsem, j, z_dev((qm + j) % 8)).start()
    loop(n_tile - LAG_CHIP, n_tile, b_step)

    sz_wait(True)
    loss_all = top + jnp.log(total) - sum_hits(stz, 8)
    bucket_is_own = bucket == qm
    line = jnp.sum(jnp.where(bucket_is_own, loss_all, 0.0), axis=0, keepdims=True)
    loss[...] = pltpu.roll(jnp.broadcast_to(line, (8, 128)), (128 - xy * 8) % 128, 1)

    grad = zk[qm]
    for j in range(1, 8):
        q = (qm + 8 - j) % 8
        remote(zr.at[q], zr.at[q], gzsem, j, z_dev(q)).wait_recv()
        part = zr[q].astype(F32)
        grad = grad + jnp.concatenate([part[:8], part[8:]], axis=1)
    gh_out[...] = grad.astype(BF16)

    for j in range(1, 8):
        q = (qm + j) % 8
        remote(zs.at[q], zr.at[qm], gzsem, j, z_dev(q)).wait_send()

    def t_sent(t):
        remote(c_send.at[t], gt_out.at[:, columns(half, t)], csem, t, other).wait_send()
        into = gt_out.at[:, columns(1 - half, t)]
        remote(c_send.at[t], into, csem, t, other).wait_recv()

    loop(0, n_tile, t_sent)


def finish(loss, gh, gt, loss_out, gh_out, gt_out, sem):
    copies = [pltpu.make_async_copy(gt, gt_out, sem.at[0]), pltpu.make_async_copy(gh, gh_out, sem.at[1])]
    for c in copies:
        c.start()
    for r in range(loss_out.shape[0]):
        loss_out[r] = loss[0, r]
    for c in copies:
        c.wait()


def on_device(hidden, item_table, bucket_blocks, targets, row_weight):
    items, feat = item_table.shape
    n_half = items // 2
    n_tile = n_half // TILE
    n_group = n_tile // GROUP
    rows = 8 * 128

    vmem = pltpu.VMEM
    dma = pltpu.SemaphoreType.DMA
    scratch = [
        vmem(hidden.shape, BF16),
        vmem(bucket_blocks.shape, jnp.int32),
        vmem((4, 128), jnp.int32),
        vmem((4, 128), F32),
        vmem((n_half, feat), BF16),
        vmem((n_group, feat, GROUP * TILE), BF16),
        vmem((16, 8, 16, 128), BF16),
        vmem((8, 128, feat), F32),
        vmem((8, feat, 128), BF16),
        vmem((feat, 128 * max(hi - lo for lo, hi in PIECES)), BF16),
        vmem((feat, rows), BF16),
        vmem((2, 16, 128), F32),
        vmem((4, 8, 128), F32),
        vmem((8, n_tile, TILE, 128), F32),
        vmem((n_tile, 8, 128), F32),
        vmem((16, 24, 128), F32),
        vmem((8, 24, 128), F32),
        vmem((GROUP * TILE, rows), BF16),
        vmem((GROUP * TILE, rows), BF16),
        vmem((feat, rows), F32),
        vmem((feat, rows), F32),
        vmem((16, 64, feat), BF16),
        vmem((16, 64, feat), BF16),
        vmem((8, 16, 128), BF16),
        vmem((8, 8, feat), F32),
        vmem((8, 16, 128), BF16),
        vmem((n_tile, 128, TILE), BF16),
        vmem((n_tile, 128, TILE), F32),
        vmem((n_tile, 128, TILE), BF16),
        vmem((n_tile, 64, TILE), BF16),
        vmem((n_tile, 64, TILE), F32),
        vmem((n_tile, 64, TILE), BF16),
        vmem((n_tile, 32, TILE), BF16),
        dma,
        dma((4,)),
        dma((2, 1)),
        dma((2, 8)),
        dma((2, 16 * len(PIECES))),
        dma((2, 16)),
        dma((2, 8)),
        dma((2, 16)),
        dma((2, 8)),
        dma((2, n_tile)),
        dma((2, n_tile)),
        dma((2, n_tile)),
        dma((2, 16)),
        dma((2, 8)),
    ]
    in_vmem = pl.BlockSpec(memory_space=pltpu.VMEM)
    in_smem = pl.BlockSpec(memory_space=pltpu.SMEM)
    anywhere = pl.BlockSpec(memory_space=pl.ANY)
    gh_shape = jax.ShapeDtypeStruct(hidden.shape, BF16)
    gt_shape = jax.ShapeDtypeStruct((feat // 8, items), BF16)
    loss, gh, gt = pl.pallas_call(
        kernel,
        out_shape=(jax.ShapeDtypeStruct((8, 128), F32), gh_shape, gt_shape),
        in_specs=[pl.BlockSpec(memory_space=pltpu.HBM)] * 5,
        out_specs=(in_vmem, in_vmem, in_vmem),
        scratch_shapes=scratch,
        compiler_params=pltpu.CompilerParams(
            collective_id=0, has_side_effects=True, vmem_limit_bytes=56 * 2**20),
    )(hidden, bucket_blocks, targets.reshape(4, 128), row_weight.reshape(4, 128), item_table)
    return pl.pallas_call(
        finish,
        out_shape=(jax.ShapeDtypeStruct((hidden.shape[0],), F32), gh_shape, gt_shape),
        in_specs=[in_smem, in_vmem, in_vmem],
        out_specs=(in_smem, anywhere, anywhere),
        scratch_shapes=[dma((2,))],
    )(loss, gh, gt)


def solution(mesh):
    in_specs = (
        P(("batch", "item"), None),
        P("item", None),
        P("batch", None),
        P("batch"),
        P("batch"),
    )
    out_specs = (P(("batch", "item")), P(("batch", "item"), None), P("batch", "item"))
    return jax.shard_map(on_device, mesh=mesh, in_specs=in_specs, out_specs=out_specs, check_vma=False)
```

```python
import functools

import jax
import jax.numpy as jnp
from jax import lax
from jax.experimental import pallas as pl
from jax.experimental.pallas import tpu as pltpu
from jax.sharding import PartitionSpec as P

MESH = pl.DeviceIdType.MESH
F32 = jnp.float32
BF16 = jnp.bfloat16

BLK = 512
NEGATIVE = -1e30
TILE = 256
GROUP = 3
LAG_CORE = 1
LAG_CHIP = 3
HIDDEN_AT = 1
EARLY = 2
REACH = (0, 1, 7, 2, 6, 3, 5, 4)
PIECES = ((0, 3), (3, 5), (5, 8))


def kernel(hid_hbm, lists_hbm, targets_hbm, weights_hbm, table, loss, gh_out, gt_out,
           hid, lists, targets, weights, tab, tab_t, hb, hf, ht, hw, hp, metab, bias, pbuf, mt, stx, stz, cbuf, obuf, ut, vt, gs, gr, zs, zk, zr,
           a_send, a_keep, a_recv, b_send, b_keep, b_recv, c_send,
           tsem, insem, msem, zsem, xsem, sxsem, szsem, hxsem, hzsem, asem, bsem, csem, gxsem, gzsem):
    b = lax.axis_index("batch")
    i = lax.axis_index("item")
    zl, k = b // 2, b % 2
    par, half = zl % 2, zl // 2
    x, zh, y = i // 16, (i // 4) % 4, i % 4
    xy = x * 4 + y
    qm = zh * 2 + half
    n_half = tab.shape[0]
    n_tile = n_half // TILE
    n_group = n_tile // GROUP

    def z_dev(q):
        return ((par + 2 * (q % 2)) * 2 + k, x * 16 + (q // 2) * 4 + y)

    def xy_dev(v):
        return (b, (v // 4) * 16 + zh * 4 + v % 4)

    sibling = (zl * 2 + 1 - k, i)
    partner = ((zl + 1 - 2 * par) * 2 + k, i)
    other = ((par + 2 * (1 - half)) * 2 + k, i)

    def remote(src, dst, sems, j, dev):
        return pltpu.make_async_remote_copy(
            src_ref=src, dst_ref=dst, send_sem=sems.at[0, j], recv_sem=sems.at[1, j],
            device_id=dev, device_id_type=MESH)

    def loop(lo, hi, body):
        def step(j, carry):
            body(j)
            return carry
        lax.fori_loop(lo, hi, step, 0)

    table_copy = pltpu.make_async_copy(table.at[pl.ds(half * n_half, n_half), :], tab, tsem)
    table_copy.start()
    inputs = [
        pltpu.make_async_copy(src, dst, insem.at[n])
        for n, (src, dst) in enumerate(
            ((hid_hbm, hid), (lists_hbm, lists), (targets_hbm, targets), (weights_hbm, weights)))
    ]
    for copy in inputs:
        copy.start()

    barrier = pltpu.get_barrier_semaphore()

    def greet(dev):
        pl.semaphore_signal(barrier, inc=1, device_id=dev, device_id_type=MESH)

    for j in (4, 3, 5, 2, 6, 1, 7):
        greet(z_dev((qm + j) % 8))
    loop(1, 16, lambda j: greet(xy_dev((xy + j) % 16)))
    greet(sibling)
    greet(partner)

    for copy in inputs:
        copy.wait()
    own = hid[...].astype(F32)
    hb[xy, 0] = jnp.concatenate([own[:, :128], own[:, 128:]], axis=0).astype(BF16)
    metab[half, 0:8, :] = lists[...].astype(F32)
    lane = lax.broadcasted_iota(jnp.int32, (1, 128), 1)
    for at, ref in ((8, targets), (12, weights)):
        rows = ref[...].astype(F32)
        turned = [rows if d == 0 else pltpu.roll(rows, 32 * d, 1) for d in range(4)]
        for to in range(4):
            line = jnp.zeros((1, 128), F32)
            for fx in range(4):
                line = jnp.where(lane // 32 == fx, turned[(fx - to) % 4][fx:fx + 1, :], line)
            metab[half, at + to:at + to + 1, :] = line
    table_copy.wait()

    def flip_group(g):
        part = tab[pl.ds(pl.multiple_of(g * GROUP * TILE, TILE), GROUP * TILE), :]
        tab_t[g] = part.astype(F32).T.astype(BF16)

    loop(0, n_group, flip_group)
    pl.semaphore_wait(barrier, 24)

    for j in (4, 3, 5, 2, 6, 1, 7):
        remote(hb.at[xy, 0], hb.at[xy, REACH.index(8 - j)], zsem, 8 - j, z_dev((qm + j) % 8)).start()
    meta_copy = remote(metab.at[half], metab.at[half], msem, 0, other)
    meta_copy.start()

    def x_copy(piece, v_from, v_to, j):
        lo, hi = PIECES[piece]
        ref = hb.at[v_from, lo:hi]
        return remote(ref, ref, xsem, piece * 16 + j, xy_dev(v_to))

    def x_send(piece):
        loop(1, 16, lambda j: x_copy(piece, xy, (xy + j) % 16, j).start())

    def z_recv(piece):
        for s in range(*PIECES[piece]):
            if s > 0:
                q = (qm + REACH[s]) % 8
                remote(hb.at[xy, s], hb.at[xy, s], zsem, REACH[s], z_dev(q)).wait_recv()

    z_recv(0)
    x_send(0)

    meta_copy.wait_send()
    remote(metab.at[1 - half], metab.at[1 - half], msem, 0, other).wait_recv()
    base = (i * 2 * n_half // BLK + half * (n_tile * TILE // BLK)).astype(F32)
    bucket = lax.broadcasted_iota(jnp.int32, (8, 128), 0)
    column = lax.broadcasted_iota(jnp.int32, (8, 128), 1) // 32
    for g in range(2):
        local = metab[g, 0:8, :] - base
        for blk in range(8):
            listed = jnp.max(jnp.where(local == blk, 1.0, 0.0), axis=1, keepdims=True)
            for side in range(2):
                spread = jnp.where(bucket == column * 2 + side, listed, 0.0)
                line = jnp.max(spread, axis=0, keepdims=True)
                bias[g * 2 + side, blk:blk + 1, :] = jnp.where(line > 0.0, 0.0, NEGATIVE)

    aim_base = (i * 2 * n_half + half * n_half).astype(F32)
    aims, weight = [], []
    for q in range(8):
        aims.append(metab[q % 2, 8 + q // 2:9 + q // 2, :] - aim_base)
        weight.append(metab[q % 2, 12 + q // 2:13 + q // 2, :])
    aim = jnp.concatenate(aims, axis=0)
    weight = jnp.concatenate(weight, axis=0)
    item_at = lax.broadcasted_iota(jnp.int32, (TILE, 128), 0).astype(F32)

    vt[...] = jnp.zeros(vt.shape, F32)

    def aim_group(g):
        for u in range(GROUP):
            here = aim - ((g * GROUP + u) * TILE).astype(F32)
            for q in range(8):
                aimed = item_at == here[q:q + 1, :]
                obuf[u * TILE:(u + 1) * TILE, q * 128:(q + 1) * 128] = jnp.where(aimed, 1.0, 0.0).astype(BF16)
        vt[...] += jnp.dot(tab_t[g], obuf[...], preferred_element_type=F32)

    for piece in range(1, len(PIECES)):
        loop(2 * piece - 2, min(2 * piece, n_group), aim_group)
        z_recv(piece)
        x_send(piece)
    loop(min(2 * len(PIECES) - 2, n_group), n_group, aim_group)

    def unpack(piece, v):
        for s in range(*PIECES[piece]):
            part = hb[v, s].astype(F32)
            rows = pl.ds(pl.multiple_of(v * 8, 8), 8)
            hf[s, rows, 0:128] = part[:8]
            hf[s, rows, 128:256] = part[8:]

    def score(piece):
        def x_recv(j):
            v = (xy + 16 - j) % 16
            x_copy(piece, v, v, j).wait_recv()
            unpack(piece, v)

        unpack(piece, xy)
        loop(1, 16, x_recv)
        places = []
        for s in range(*PIECES[piece]):
            q = (qm + REACH[s]) % 8
            flat = hf[s].T.astype(BF16)
            ht[q] = flat
            hw[:, len(places) * 128:(len(places) + 1) * 128] = flat
            places.append((q, (q % 2) * 2 + q // 4))
        scores = jnp.dot(tab[...], hw[:, 0:len(places) * 128], preferred_element_type=F32)
        tops = [[] for _ in places]
        sums = [[] for _ in places]
        for t in range(n_tile):
            for at, (q, side) in enumerate(places):
                s = scores[t * TILE:(t + 1) * TILE, at * 128:(at + 1) * 128]
                top = jnp.max(s, axis=0, keepdims=True)
                e = jnp.exp(s - top)
                pbuf[q, t] = e
                top = top + bias[side, pl.ds((t + half) // 2, 1), :]
                mt[t, pl.ds(q, 1), :] = top
                tops[at].append(top)
                sums[at].append(jnp.sum(e, axis=0, keepdims=True))
        for at, (q, side) in enumerate(places):
            top = functools.reduce(jnp.maximum, tops[at])
            stx[xy, pl.ds(q, 1), :] = top
            stx[xy, pl.ds(8 + q, 1), :] = sum(n * jnp.exp(m - top) for n, m in zip(sums[at], tops[at]))

    for piece in range(len(PIECES)):
        score(piece)

    def sx_copy(hits, j, v_from, v_to):
        ref = stx.at[v_from, 16:24] if hits else stx.at[v_from, 0:16]
        return remote(ref, ref, hxsem if hits else sxsem, j, xy_dev(v_to))

    def sz_copy(hits, j, q_from, q_to):
        ref = stz.at[q_from, 16:24] if hits else stz.at[q_from, 0:16]
        return remote(ref, ref, hzsem if hits else szsem, j, z_dev(q_to))

    loop(1, 16, lambda j: sx_copy(False, j, xy, (xy + j) % 16).start())
    top_here = stx[xy, 0:8, :]
    for q in range(8):
        at = slice(q * 128, (q + 1) * 128)
        stx[xy, 16 + q:17 + q, :] = jnp.sum(ht[q].astype(F32) * vt[:, at], axis=0, keepdims=True)
    hit_here = stx[xy, 16:24, :]
    loop(1, 16, lambda j: sx_copy(True, j, xy, (xy + j) % 16).start())

    for rel in range(8):
        to = (par + (rel // 2) % 2) % 2 + 2 * ((half + rel % 2) % 2)
        f0 = pl.multiple_of((to * 2 + (k + rel // 4) % 2) * 32, 32)
        for q in range(8):
            hp[rel * 32:(rel + 1) * 32, q * 128:(q + 1) * 128] = ht[q, pl.ds(f0, 32), :]

    ut[...] = jnp.zeros(ut.shape, F32)

    def early_group(g):
        for u in range(GROUP):
            t = g * GROUP + u
            here = aim - (t * TILE).astype(F32)
            factor = jnp.exp(mt[t] - top_here)
            for q in range(8):
                at = slice(q * 128, (q + 1) * 128)
                aimed = item_at == here[q:q + 1, :]
                cbuf[u * TILE:(u + 1) * TILE, at] = jnp.where(aimed, 0.0, pbuf[q, t] * factor[q:q + 1, :]).astype(BF16)
        ut[...] += jnp.dot(tab_t[g], cbuf[...], preferred_element_type=F32)

    loop(0, EARLY, early_group)

    def merge(ref, n):
        top = ref[0, 0:8, :]
        for v in range(1, n):
            top = jnp.maximum(top, ref[v, 0:8, :])
        total = jnp.zeros_like(top)
        for v in range(n):
            total = total + ref[v, 8:16, :] * jnp.exp(ref[v, 0:8, :] - top)
        return top, total

    def sum_hits(ref, n):
        hit = ref[0, 16:24, :]
        for v in range(1, n):
            hit = hit + ref[v, 16:24, :]
        return hit

    def sx_wait(hits):
        def wait(j):
            v = (xy + 16 - j) % 16
            sx_copy(hits, j, v, v).wait_recv()
        loop(1, 16, wait)

    def sz_wait(hits):
        for j in range(1, 8):
            q = (qm + 8 - j) % 8
            sz_copy(hits, j, q, q).wait_recv()

    sx_wait(False)
    top, total = merge(stx, 16)
    stz[qm, 0:8, :] = top
    stz[qm, 8:16, :] = total
    for j in (4, 3, 5, 2, 6, 1, 7):
        sz_copy(False, j, qm, (qm + j) % 8).start()
    loop(EARLY, n_group, early_group)
    sx_wait(True)
    stz[qm, 16:24, :] = sum_hits(stx, 16)
    for j in (4, 3, 5, 2, 6, 1, 7):
        sz_copy(True, j, qm, (qm + j) % 8).start()

    def x_sent(j):
        v = (xy + j) % 16
        for piece in range(len(PIECES)):
            x_copy(piece, xy, v, j).wait_send()
        sx_copy(False, j, xy, v).wait_send()
        sx_copy(True, j, xy, v).wait_send()

    loop(1, 16, x_sent)
    for j in range(1, 8):
        q = (qm + j) % 8
        remote(hb.at[xy, 0], hb.at[xy, REACH.index(8 - j)], zsem, 8 - j, z_dev(q)).wait_send()
        sz_copy(False, j, qm, q).wait_send()
        sz_copy(True, j, qm, q).wait_send()
    sz_wait(False)
    top, total = merge(stz, 8)
    scale = weight / total

    def a_step(t):
        remote(a_send.at[t], a_recv.at[t], asem, t, sibling).wait()
        summed = a_keep[t] + a_recv[t].astype(F32)
        b_send[t] = summed[64:].astype(BF16)
        b_keep[t] = summed[:64]
        remote(b_send.at[t], b_recv.at[t], bsem, t, partner).start()

    def columns(which, t):
        return pl.ds(pl.multiple_of(which * n_half + t * GROUP * TILE, TILE), GROUP * TILE)

    def b_step(t):
        remote(b_send.at[t], b_recv.at[t], bsem, t, partner).wait()
        summed = (b_keep[t] + b_recv[t].astype(F32)).astype(BF16)
        c_send[t] = summed[32:]
        gt_out[:, columns(half, t)] = summed[:32]
        remote(c_send.at[t], gt_out.at[:, columns(half, t)], csem, t, other).start()

    def grad_group(t):
        for u in range(GROUP):
            here = aim - ((t * GROUP + u) * TILE).astype(F32)
            factor = jnp.exp(mt[t * GROUP + u] - top) * scale
            for q in range(8):
                less = jnp.where(item_at == here[q:q + 1, :], weight[q:q + 1, :], 0.0)
                coef = pbuf[q, t * GROUP + u] * factor[q:q + 1, :] - less
                cbuf[u * TILE:(u + 1) * TILE, q * 128:(q + 1) * 128] = coef.astype(BF16)
        g = lax.dot_general(hp[...], cbuf[...], (((1,), (1,)), ((), ())), preferred_element_type=F32)
        a_send[t] = g[128:].astype(BF16)
        a_keep[t] = g[:128]
        remote(a_send.at[t], a_recv.at[t], asem, t, sibling).start()

        @pl.when(t >= LAG_CORE)
        def _():
            a_step(t - LAG_CORE)

        @pl.when(t >= LAG_CHIP)
        def _():
            b_step(t - LAG_CHIP)

    loop(0, HIDDEN_AT, grad_group)

    on_here = (aim >= 0.0) & (aim < float(n_half))
    chance = jnp.exp(jnp.where(on_here, hit_here, NEGATIVE) - top) / total
    of_target = weight * (chance - 1.0)
    of_rest = jnp.exp(top_here - top) * scale
    for q in range(8):
        at = slice(q * 128, (q + 1) * 128)
        grad = ut[:, at] * of_rest[q:q + 1, :] + vt[:, at] * of_target[q:q + 1, :]
        hf[q] = grad.T

    def gather_rows(v):
        rows = pl.ds(pl.multiple_of(v * 8, 8), 8)
        return jnp.concatenate([hf[q, rows, :] for q in range(8)], axis=0)

    def g_send(j):
        v = (xy + j) % 16
        gs[v] = gather_rows(v).astype(BF16)
        remote(gs.at[v], gr.at[xy], gxsem, j, xy_dev(v)).start()

    loop(1, 16, g_send)
    mine = gather_rows(xy)
    loop(HIDDEN_AT, n_group, grad_group)
    loop(n_group - LAG_CORE, n_group, a_step)
    def gx_recv(j, total):
        v = (xy + 16 - j) % 16
        remote(gr.at[v], gr.at[v], gxsem, j, xy_dev(v)).wait_recv()
        to = (xy + j) % 16
        remote(gs.at[to], gr.at[xy], gxsem, j, xy_dev(to)).wait_send()
        return total + gr[v].astype(F32)

    summed = lax.fori_loop(1, 16, gx_recv, mine)
    for q in range(8):
        part = summed[q * 8:(q + 1) * 8, :]
        zs[q] = jnp.concatenate([part[:, :128], part[:, 128:]], axis=0).astype(BF16)
        zk[q] = part
    for j in (4, 3, 5, 2, 6, 1, 7):
        remote(zs.at[(qm + j) % 8], zr.at[qm], gzsem, j, z_dev((qm + j) % 8)).start()
    loop(n_group - LAG_CHIP, n_group, b_step)

    sz_wait(True)
    loss_all = top + jnp.log(total) - sum_hits(stz, 8)
    bucket_is_own = bucket == qm
    line = jnp.sum(jnp.where(bucket_is_own, loss_all, 0.0), axis=0, keepdims=True)
    loss[...] = pltpu.roll(jnp.broadcast_to(line, (8, 128)), (128 - xy * 8) % 128, 1)

    grad = zk[qm]
    for j in range(1, 8):
        q = (qm + 8 - j) % 8
        remote(zr.at[q], zr.at[q], gzsem, j, z_dev(q)).wait_recv()
        part = zr[q].astype(F32)
        grad = grad + jnp.concatenate([part[:8], part[8:]], axis=1)
    gh_out[...] = grad.astype(BF16)

    for j in range(1, 8):
        q = (qm + j) % 8
        remote(zs.at[q], zr.at[qm], gzsem, j, z_dev(q)).wait_send()

    def t_sent(t):
        remote(c_send.at[t], gt_out.at[:, columns(half, t)], csem, t, other).wait_send()
        into = gt_out.at[:, columns(1 - half, t)]
        remote(c_send.at[t], into, csem, t, other).wait_recv()

    loop(0, n_group, t_sent)


def finish(loss, gh, gt, loss_out, gh_out, gt_out, sem):
    copies = [pltpu.make_async_copy(gt, gt_out, sem.at[0]), pltpu.make_async_copy(gh, gh_out, sem.at[1])]
    for c in copies:
        c.start()
    for r in range(loss_out.shape[0]):
        loss_out[r] = loss[0, r]
    for c in copies:
        c.wait()


def on_device(hidden, item_table, bucket_blocks, targets, row_weight):
    items, feat = item_table.shape
    n_half = items // 2
    n_tile = n_half // TILE
    n_group = n_tile // GROUP
    rows = 8 * 128

    vmem = pltpu.VMEM
    dma = pltpu.SemaphoreType.DMA
    scratch = [
        vmem(hidden.shape, BF16),
        vmem(bucket_blocks.shape, jnp.int32),
        vmem((4, 128), jnp.int32),
        vmem((4, 128), F32),
        vmem((n_half, feat), BF16),
        vmem((n_group, feat, GROUP * TILE), BF16),
        vmem((16, 8, 16, 128), BF16),
        vmem((8, 128, feat), F32),
        vmem((8, feat, 128), BF16),
        vmem((feat, 128 * max(hi - lo for lo, hi in PIECES)), BF16),
        vmem((feat, rows), BF16),
        vmem((2, 16, 128), F32),
        vmem((4, 8, 128), F32),
        vmem((8, n_tile, TILE, 128), F32),
        vmem((n_tile, 8, 128), F32),
        vmem((16, 24, 128), F32),
        vmem((8, 24, 128), F32),
        vmem((GROUP * TILE, rows), BF16),
        vmem((GROUP * TILE, rows), BF16),
        vmem((feat, rows), F32),
        vmem((feat, rows), F32),
        vmem((16, 64, feat), BF16),
        vmem((16, 64, feat), BF16),
        vmem((8, 16, 128), BF16),
        vmem((8, 8, feat), F32),
        vmem((8, 16, 128), BF16),
        vmem((n_group, 128, GROUP * TILE), BF16),
        vmem((n_group, 128, GROUP * TILE), F32),
        vmem((n_group, 128, GROUP * TILE), BF16),
        vmem((n_group, 64, GROUP * TILE), BF16),
        vmem((n_group, 64, GROUP * TILE), F32),
        vmem((n_group, 64, GROUP * TILE), BF16),
        vmem((n_group, 32, GROUP * TILE), BF16),
        dma,
        dma((4,)),
        dma((2, 1)),
        dma((2, 8)),
        dma((2, 16 * len(PIECES))),
        dma((2, 16)),
        dma((2, 8)),
        dma((2, 16)),
        dma((2, 8)),
        dma((2, n_group)),
        dma((2, n_group)),
        dma((2, n_group)),
        dma((2, 16)),
        dma((2, 8)),
    ]
    in_vmem = pl.BlockSpec(memory_space=pltpu.VMEM)
    in_smem = pl.BlockSpec(memory_space=pltpu.SMEM)
    anywhere = pl.BlockSpec(memory_space=pl.ANY)
    gh_shape = jax.ShapeDtypeStruct(hidden.shape, BF16)
    gt_shape = jax.ShapeDtypeStruct((feat // 8, items), BF16)
    loss, gh, gt = pl.pallas_call(
        kernel,
        out_shape=(jax.ShapeDtypeStruct((8, 128), F32), gh_shape, gt_shape),
        in_specs=[pl.BlockSpec(memory_space=pltpu.HBM)] * 5,
        out_specs=(in_vmem, in_vmem, in_vmem),
        scratch_shapes=scratch,
        compiler_params=pltpu.CompilerParams(
            collective_id=0, has_side_effects=True, vmem_limit_bytes=56 * 2**20),
    )(hidden, bucket_blocks, targets.reshape(4, 128), row_weight.reshape(4, 128), item_table)
    return pl.pallas_call(
        finish,
        out_shape=(jax.ShapeDtypeStruct((hidden.shape[0],), F32), gh_shape, gt_shape),
        in_specs=[in_smem, in_vmem, in_vmem],
        out_specs=(in_smem, anywhere, anywhere),
        scratch_shapes=[dma((2,))],
    )(loss, gh, gt)


def solution(mesh):
    in_specs = (
        P(("batch", "item"), None),
        P("item", None),
        P("batch", None),
        P("batch"),
        P("batch"),
    )
    out_specs = (P(("batch", "item")), P(("batch", "item"), None), P("batch", "item"))
    return jax.shard_map(on_device, mesh=mesh, in_specs=in_specs, out_specs=out_specs, check_vma=False)
```

```python
import functools

import jax
import jax.numpy as jnp
from jax import lax
from jax.experimental import pallas as pl
from jax.experimental.pallas import tpu as pltpu
from jax.sharding import PartitionSpec as P

MESH = pl.DeviceIdType.MESH
F32 = jnp.float32
BF16 = jnp.bfloat16

BLK = 512
NEGATIVE = -1e30
TILE = 256
GROUP = 3
LAG_CORE = 1
LAG_CHIP = 3
HIDDEN_AT = 1
EARLY = 3
REACH = (0, 1, 7, 2, 6, 3, 5, 4)
PIECES = ((0, 3), (3, 5), (5, 8))


def kernel(hid_hbm, lists_hbm, targets_hbm, weights_hbm, table, loss, gh_out, gt_out,
           hid, lists, targets, weights, tab, tab_t, hb, hf, ht, hw, hp, metab, bias, pbuf, mt, stx, stz, cbuf, obuf, ut, vt, gs, gr, zs, zk, zr,
           a_send, a_keep, a_recv, b_send, b_keep, b_recv, c_send,
           tsem, insem, msem, zsem, xsem, sxsem, szsem, hxsem, hzsem, asem, bsem, csem, gxsem, gzsem):
    b = lax.axis_index("batch")
    i = lax.axis_index("item")
    zl, k = b // 2, b % 2
    par, half = zl % 2, zl // 2
    x, zh, y = i // 16, (i // 4) % 4, i % 4
    xy = x * 4 + y
    qm = zh * 2 + half
    n_half = tab.shape[0]
    n_tile = n_half // TILE
    n_group = n_tile // GROUP

    def z_dev(q):
        return ((par + 2 * (q % 2)) * 2 + k, x * 16 + (q // 2) * 4 + y)

    def xy_dev(v):
        return (b, (v // 4) * 16 + zh * 4 + v % 4)

    sibling = (zl * 2 + 1 - k, i)
    partner = ((zl + 1 - 2 * par) * 2 + k, i)
    other = ((par + 2 * (1 - half)) * 2 + k, i)

    def remote(src, dst, sems, j, dev):
        return pltpu.make_async_remote_copy(
            src_ref=src, dst_ref=dst, send_sem=sems.at[0, j], recv_sem=sems.at[1, j],
            device_id=dev, device_id_type=MESH)

    def loop(lo, hi, body):
        def step(j, carry):
            body(j)
            return carry
        lax.fori_loop(lo, hi, step, 0)

    table_copy = pltpu.make_async_copy(table.at[pl.ds(half * n_half, n_half), :], tab, tsem)
    table_copy.start()
    inputs = [
        pltpu.make_async_copy(src, dst, insem.at[n])
        for n, (src, dst) in enumerate(
            ((hid_hbm, hid), (lists_hbm, lists), (targets_hbm, targets), (weights_hbm, weights)))
    ]
    for copy in inputs:
        copy.start()

    barrier = pltpu.get_barrier_semaphore()

    def greet(dev):
        pl.semaphore_signal(barrier, inc=1, device_id=dev, device_id_type=MESH)

    for j in (4, 3, 5, 2, 6, 1, 7):
        greet(z_dev((qm + j) % 8))
    loop(1, 16, lambda j: greet(xy_dev((xy + j) % 16)))
    greet(sibling)
    greet(partner)

    for copy in inputs:
        copy.wait()
    own = hid[...].astype(F32)
    hb[xy, 0] = jnp.concatenate([own[:, :128], own[:, 128:]], axis=0).astype(BF16)
    metab[half, 0:8, :] = lists[...].astype(F32)
    lane = lax.broadcasted_iota(jnp.int32, (1, 128), 1)
    for at, ref in ((8, targets), (12, weights)):
        rows = ref[...].astype(F32)
        turned = [rows if d == 0 else pltpu.roll(rows, 32 * d, 1) for d in range(4)]
        for to in range(4):
            line = jnp.zeros((1, 128), F32)
            for fx in range(4):
                line = jnp.where(lane // 32 == fx, turned[(fx - to) % 4][fx:fx + 1, :], line)
            metab[half, at + to:at + to + 1, :] = line
    table_copy.wait()

    def flip_group(g):
        part = tab[pl.ds(pl.multiple_of(g * GROUP * TILE, TILE), GROUP * TILE), :]
        tab_t[g] = part.astype(F32).T.astype(BF16)

    loop(0, n_group, flip_group)
    pl.semaphore_wait(barrier, 24)

    for j in (4, 3, 5, 2, 6, 1, 7):
        remote(hb.at[xy, 0], hb.at[xy, REACH.index(8 - j)], zsem, 8 - j, z_dev((qm + j) % 8)).start()
    meta_copy = remote(metab.at[half], metab.at[half], msem, 0, other)
    meta_copy.start()

    def x_copy(piece, v_from, v_to, j):
        lo, hi = PIECES[piece]
        ref = hb.at[v_from, lo:hi]
        return remote(ref, ref, xsem, piece * 16 + j, xy_dev(v_to))

    def x_send(piece):
        loop(1, 16, lambda j: x_copy(piece, xy, (xy + j) % 16, j).start())

    def z_recv(piece):
        for s in range(*PIECES[piece]):
            if s > 0:
                q = (qm + REACH[s]) % 8
                remote(hb.at[xy, s], hb.at[xy, s], zsem, REACH[s], z_dev(q)).wait_recv()

    z_recv(0)
    x_send(0)

    meta_copy.wait_send()
    remote(metab.at[1 - half], metab.at[1 - half], msem, 0, other).wait_recv()
    base = (i * 2 * n_half // BLK + half * (n_tile * TILE // BLK)).astype(F32)
    bucket = lax.broadcasted_iota(jnp.int32, (8, 128), 0)
    column = lax.broadcasted_iota(jnp.int32, (8, 128), 1) // 32
    for g in range(2):
        local = metab[g, 0:8, :] - base
        for blk in range(8):
            listed = jnp.max(jnp.where(local == blk, 1.0, 0.0), axis=1, keepdims=True)
            for side in range(2):
                spread = jnp.where(bucket == column * 2 + side, listed, 0.0)
                line = jnp.max(spread, axis=0, keepdims=True)
                bias[g * 2 + side, blk:blk + 1, :] = jnp.where(line > 0.0, 0.0, NEGATIVE)

    aim_base = (i * 2 * n_half + half * n_half).astype(F32)
    aims, weight = [], []
    for q in range(8):
        aims.append(metab[q % 2, 8 + q // 2:9 + q // 2, :] - aim_base)
        weight.append(metab[q % 2, 12 + q // 2:13 + q // 2, :])
    aim = jnp.concatenate(aims, axis=0)
    weight = jnp.concatenate(weight, axis=0)
    item_at = lax.broadcasted_iota(jnp.int32, (TILE, 128), 0).astype(F32)

    vt[...] = jnp.zeros(vt.shape, F32)

    def aim_group(g):
        for u in range(GROUP):
            here = aim - ((g * GROUP + u) * TILE).astype(F32)
            for q in range(8):
                aimed = item_at == here[q:q + 1, :]
                obuf[u * TILE:(u + 1) * TILE, q * 128:(q + 1) * 128] = jnp.where(aimed, 1.0, 0.0).astype(BF16)
        vt[...] += jnp.dot(tab_t[g], obuf[...], preferred_element_type=F32)

    for piece in range(1, len(PIECES)):
        loop(2 * piece - 2, min(2 * piece, n_group), aim_group)
        z_recv(piece)
        x_send(piece)
    loop(min(2 * len(PIECES) - 2, n_group), n_group, aim_group)

    def unpack(piece, v):
        for s in range(*PIECES[piece]):
            part = hb[v, s].astype(F32)
            rows = pl.ds(pl.multiple_of(v * 8, 8), 8)
            hf[s, rows, 0:128] = part[:8]
            hf[s, rows, 128:256] = part[8:]

    def score(piece):
        def x_recv(j):
            v = (xy + 16 - j) % 16
            x_copy(piece, v, v, j).wait_recv()
            unpack(piece, v)

        unpack(piece, xy)
        loop(1, 16, x_recv)
        places = []
        for s in range(*PIECES[piece]):
            q = (qm + REACH[s]) % 8
            flat = hf[s].T.astype(BF16)
            ht[q] = flat
            hw[:, len(places) * 128:(len(places) + 1) * 128] = flat
            places.append((q, (q % 2) * 2 + q // 4))
        scores = jnp.dot(tab[...], hw[:, 0:len(places) * 128], preferred_element_type=F32)
        tops = [[] for _ in places]
        sums = [[] for _ in places]
        for t in range(n_tile):
            for at, (q, side) in enumerate(places):
                s = scores[t * TILE:(t + 1) * TILE, at * 128:(at + 1) * 128]
                top = jnp.max(s, axis=0, keepdims=True)
                e = jnp.exp(s - top)
                pbuf[q, t] = e
                top = top + bias[side, pl.ds((t + half) // 2, 1), :]
                mt[t, pl.ds(q, 1), :] = top
                tops[at].append(top)
                sums[at].append(jnp.sum(e, axis=0, keepdims=True))
        for at, (q, side) in enumerate(places):
            top = functools.reduce(jnp.maximum, tops[at])
            stx[xy, pl.ds(q, 1), :] = top
            stx[xy, pl.ds(8 + q, 1), :] = sum(n * jnp.exp(m - top) for n, m in zip(sums[at], tops[at]))

    for piece in range(len(PIECES)):
        score(piece)

    def sx_copy(hits, j, v_from, v_to):
        ref = stx.at[v_from, 16:24] if hits else stx.at[v_from, 0:16]
        return remote(ref, ref, hxsem if hits else sxsem, j, xy_dev(v_to))

    def sz_copy(hits, j, q_from, q_to):
        ref = stz.at[q_from, 16:24] if hits else stz.at[q_from, 0:16]
        return remote(ref, ref, hzsem if hits else szsem, j, z_dev(q_to))

    loop(1, 16, lambda j: sx_copy(False, j, xy, (xy + j) % 16).start())
    top_here = stx[xy, 0:8, :]
    for q in range(8):
        at = slice(q * 128, (q + 1) * 128)
        stx[xy, 16 + q:17 + q, :] = jnp.sum(ht[q].astype(F32) * vt[:, at], axis=0, keepdims=True)
    hit_here = stx[xy, 16:24, :]
    loop(1, 16, lambda j: sx_copy(True, j, xy, (xy + j) % 16).start())

    for rel in range(8):
        to = (par + (rel // 2) % 2) % 2 + 2 * ((half + rel % 2) % 2)
        f0 = pl.multiple_of((to * 2 + (k + rel // 4) % 2) * 32, 32)
        for q in range(8):
            hp[rel * 32:(rel + 1) * 32, q * 128:(q + 1) * 128] = ht[q, pl.ds(f0, 32), :]

    ut[...] = jnp.zeros(ut.shape, F32)

    def early_group(g):
        for u in range(GROUP):
            t = g * GROUP + u
            here = aim - (t * TILE).astype(F32)
            factor = jnp.exp(mt[t] - top_here)
            for q in range(8):
                at = slice(q * 128, (q + 1) * 128)
                aimed = item_at == here[q:q + 1, :]
                cbuf[u * TILE:(u + 1) * TILE, at] = jnp.where(aimed, 0.0, pbuf[q, t] * factor[q:q + 1, :]).astype(BF16)
        ut[...] += jnp.dot(tab_t[g], cbuf[...], preferred_element_type=F32)

    loop(0, EARLY, early_group)

    def merge(ref, n):
        top = ref[0, 0:8, :]
        for v in range(1, n):
            top = jnp.maximum(top, ref[v, 0:8, :])
        total = jnp.zeros_like(top)
        for v in range(n):
            total = total + ref[v, 8:16, :] * jnp.exp(ref[v, 0:8, :] - top)
        return top, total

    def sum_hits(ref, n):
        hit = ref[0, 16:24, :]
        for v in range(1, n):
            hit = hit + ref[v, 16:24, :]
        return hit

    def sx_wait(hits):
        def wait(j):
            v = (xy + 16 - j) % 16
            sx_copy(hits, j, v, v).wait_recv()
        loop(1, 16, wait)

    def sz_wait(hits):
        for j in range(1, 8):
            q = (qm + 8 - j) % 8
            sz_copy(hits, j, q, q).wait_recv()

    sx_wait(False)
    top, total = merge(stx, 16)
    stz[qm, 0:8, :] = top
    stz[qm, 8:16, :] = total
    for j in (4, 3, 5, 2, 6, 1, 7):
        sz_copy(False, j, qm, (qm + j) % 8).start()
    loop(EARLY, n_group, early_group)
    sx_wait(True)
    stz[qm, 16:24, :] = sum_hits(stx, 16)
    for j in (4, 3, 5, 2, 6, 1, 7):
        sz_copy(True, j, qm, (qm + j) % 8).start()

    def x_sent(j):
        v = (xy + j) % 16
        for piece in range(len(PIECES)):
            x_copy(piece, xy, v, j).wait_send()
        sx_copy(False, j, xy, v).wait_send()
        sx_copy(True, j, xy, v).wait_send()

    loop(1, 16, x_sent)
    for j in range(1, 8):
        q = (qm + j) % 8
        remote(hb.at[xy, 0], hb.at[xy, REACH.index(8 - j)], zsem, 8 - j, z_dev(q)).wait_send()
        sz_copy(False, j, qm, q).wait_send()
        sz_copy(True, j, qm, q).wait_send()
    sz_wait(False)
    top, total = merge(stz, 8)
    scale = weight / total

    def a_step(t):
        remote(a_send.at[t], a_recv.at[t], asem, t, sibling).wait()
        summed = a_keep[t] + a_recv[t].astype(F32)
        b_send[t] = summed[64:].astype(BF16)
        b_keep[t] = summed[:64]
        remote(b_send.at[t], b_recv.at[t], bsem, t, partner).start()

    def columns(which, t):
        return pl.ds(pl.multiple_of(which * n_half + t * GROUP * TILE, TILE), GROUP * TILE)

    def b_step(t):
        remote(b_send.at[t], b_recv.at[t], bsem, t, partner).wait()
        summed = (b_keep[t] + b_recv[t].astype(F32)).astype(BF16)
        c_send[t] = summed[32:]
        gt_out[:, columns(half, t)] = summed[:32]
        remote(c_send.at[t], gt_out.at[:, columns(half, t)], csem, t, other).start()

    def grad_group(t):
        for u in range(GROUP):
            here = aim - ((t * GROUP + u) * TILE).astype(F32)
            factor = jnp.exp(mt[t * GROUP + u] - top) * scale
            for q in range(8):
                less = jnp.where(item_at == here[q:q + 1, :], weight[q:q + 1, :], 0.0)
                coef = pbuf[q, t * GROUP + u] * factor[q:q + 1, :] - less
                cbuf[u * TILE:(u + 1) * TILE, q * 128:(q + 1) * 128] = coef.astype(BF16)
        g = lax.dot_general(hp[...], cbuf[...], (((1,), (1,)), ((), ())), preferred_element_type=F32)
        a_send[t] = g[128:].astype(BF16)
        a_keep[t] = g[:128]
        remote(a_send.at[t], a_recv.at[t], asem, t, sibling).start()

        @pl.when(t >= LAG_CORE)
        def _():
            a_step(t - LAG_CORE)

        @pl.when(t >= LAG_CHIP)
        def _():
            b_step(t - LAG_CHIP)

    loop(0, HIDDEN_AT, grad_group)

    on_here = (aim >= 0.0) & (aim < float(n_half))
    chance = jnp.exp(jnp.where(on_here, hit_here, NEGATIVE) - top) / total
    of_target = weight * (chance - 1.0)
    of_rest = jnp.exp(top_here - top) * scale
    for q in range(8):
        at = slice(q * 128, (q + 1) * 128)
        grad = ut[:, at] * of_rest[q:q + 1, :] + vt[:, at] * of_target[q:q + 1, :]
        hf[q] = grad.T

    def gather_rows(v):
        rows = pl.ds(pl.multiple_of(v * 8, 8), 8)
        return jnp.concatenate([hf[q, rows, :] for q in range(8)], axis=0)

    def g_send(j):
        v = (xy + j) % 16
        gs[v] = gather_rows(v).astype(BF16)
        remote(gs.at[v], gr.at[xy], gxsem, j, xy_dev(v)).start()

    loop(1, 16, g_send)
    mine = gather_rows(xy)
    loop(HIDDEN_AT, n_group, grad_group)
    loop(n_group - LAG_CORE, n_group, a_step)
    def gx_recv(j, total):
        v = (xy + 16 - j) % 16
        remote(gr.at[v], gr.at[v], gxsem, j, xy_dev(v)).wait_recv()
        to = (xy + j) % 16
        remote(gs.at[to], gr.at[xy], gxsem, j, xy_dev(to)).wait_send()
        return total + gr[v].astype(F32)

    summed = lax.fori_loop(1, 16, gx_recv, mine)
    for q in range(8):
        part = summed[q * 8:(q + 1) * 8, :]
        zs[q] = jnp.concatenate([part[:, :128], part[:, 128:]], axis=0).astype(BF16)
        zk[q] = part
    for j in (4, 3, 5, 2, 6, 1, 7):
        remote(zs.at[(qm + j) % 8], zr.at[qm], gzsem, j, z_dev((qm + j) % 8)).start()
    loop(n_group - LAG_CHIP, n_group, b_step)

    sz_wait(True)
    loss_all = top + jnp.log(total) - sum_hits(stz, 8)
    bucket_is_own = bucket == qm
    line = jnp.sum(jnp.where(bucket_is_own, loss_all, 0.0), axis=0, keepdims=True)
    loss[...] = pltpu.roll(jnp.broadcast_to(line, (8, 128)), (128 - xy * 8) % 128, 1)

    grad = zk[qm]
    for j in range(1, 8):
        q = (qm + 8 - j) % 8
        remote(zr.at[q], zr.at[q], gzsem, j, z_dev(q)).wait_recv()
        part = zr[q].astype(F32)
        grad = grad + jnp.concatenate([part[:8], part[8:]], axis=1)
    gh_out[...] = grad.astype(BF16)

    for j in range(1, 8):
        q = (qm + j) % 8
        remote(zs.at[q], zr.at[qm], gzsem, j, z_dev(q)).wait_send()

    def t_sent(t):
        remote(c_send.at[t], gt_out.at[:, columns(half, t)], csem, t, other).wait_send()
        into = gt_out.at[:, columns(1 - half, t)]
        remote(c_send.at[t], into, csem, t, other).wait_recv()

    loop(0, n_group, t_sent)


def finish(loss, gh, gt, loss_out, gh_out, gt_out, sem):
    copies = [pltpu.make_async_copy(gt, gt_out, sem.at[0]), pltpu.make_async_copy(gh, gh_out, sem.at[1])]
    for c in copies:
        c.start()
    for r in range(loss_out.shape[0]):
        loss_out[r] = loss[0, r]
    for c in copies:
        c.wait()


def on_device(hidden, item_table, bucket_blocks, targets, row_weight):
    items, feat = item_table.shape
    n_half = items // 2
    n_tile = n_half // TILE
    n_group = n_tile // GROUP
    rows = 8 * 128

    vmem = pltpu.VMEM
    dma = pltpu.SemaphoreType.DMA
    scratch = [
        vmem(hidden.shape, BF16),
        vmem(bucket_blocks.shape, jnp.int32),
        vmem((4, 128), jnp.int32),
        vmem((4, 128), F32),
        vmem((n_half, feat), BF16),
        vmem((n_group, feat, GROUP * TILE), BF16),
        vmem((16, 8, 16, 128), BF16),
        vmem((8, 128, feat), F32),
        vmem((8, feat, 128), BF16),
        vmem((feat, 128 * max(hi - lo for lo, hi in PIECES)), BF16),
        vmem((feat, rows), BF16),
        vmem((2, 16, 128), F32),
        vmem((4, 8, 128), F32),
        vmem((8, n_tile, TILE, 128), F32),
        vmem((n_tile, 8, 128), F32),
        vmem((16, 24, 128), F32),
        vmem((8, 24, 128), F32),
        vmem((GROUP * TILE, rows), BF16),
        vmem((GROUP * TILE, rows), BF16),
        vmem((feat, rows), F32),
        vmem((feat, rows), F32),
        vmem((16, 64, feat), BF16),
        vmem((16, 64, feat), BF16),
        vmem((8, 16, 128), BF16),
        vmem((8, 8, feat), F32),
        vmem((8, 16, 128), BF16),
        vmem((n_group, 128, GROUP * TILE), BF16),
        vmem((n_group, 128, GROUP * TILE), F32),
        vmem((n_group, 128, GROUP * TILE), BF16),
        vmem((n_group, 64, GROUP * TILE), BF16),
        vmem((n_group, 64, GROUP * TILE), F32),
        vmem((n_group, 64, GROUP * TILE), BF16),
        vmem((n_group, 32, GROUP * TILE), BF16),
        dma,
        dma((4,)),
        dma((2, 1)),
        dma((2, 8)),
        dma((2, 16 * len(PIECES))),
        dma((2, 16)),
        dma((2, 8)),
        dma((2, 16)),
        dma((2, 8)),
        dma((2, n_group)),
        dma((2, n_group)),
        dma((2, n_group)),
        dma((2, 16)),
        dma((2, 8)),
    ]
    in_vmem = pl.BlockSpec(memory_space=pltpu.VMEM)
    in_smem = pl.BlockSpec(memory_space=pltpu.SMEM)
    anywhere = pl.BlockSpec(memory_space=pl.ANY)
    gh_shape = jax.ShapeDtypeStruct(hidden.shape, BF16)
    gt_shape = jax.ShapeDtypeStruct((feat // 8, items), BF16)
    loss, gh, gt = pl.pallas_call(
        kernel,
        out_shape=(jax.ShapeDtypeStruct((8, 128), F32), gh_shape, gt_shape),
        in_specs=[pl.BlockSpec(memory_space=pltpu.HBM)] * 5,
        out_specs=(in_vmem, in_vmem, in_vmem),
        scratch_shapes=scratch,
        compiler_params=pltpu.CompilerParams(
            collective_id=0, has_side_effects=True, vmem_limit_bytes=56 * 2**20),
    )(hidden, bucket_blocks, targets.reshape(4, 128), row_weight.reshape(4, 128), item_table)
    return pl.pallas_call(
        finish,
        out_shape=(jax.ShapeDtypeStruct((hidden.shape[0],), F32), gh_shape, gt_shape),
        in_specs=[in_smem, in_vmem, in_vmem],
        out_specs=(in_smem, anywhere, anywhere),
        scratch_shapes=[dma((2,))],
    )(loss, gh, gt)


def solution(mesh):
    in_specs = (
        P(("batch", "item"), None),
        P("item", None),
        P("batch", None),
        P("batch"),
        P("batch"),
    )
    out_specs = (P(("batch", "item")), P(("batch", "item"), None), P("batch", "item"))
    return jax.shard_map(on_device, mesh=mesh, in_specs=in_specs, out_specs=out_specs, check_vma=False)
```
